128 devices in a mesh: gx: 16 (over z_lo, x, core), gy: 8 (over z_hi, y).
Axes of the slice: x: 4, y: 4, z: 4 (z_hi: 2, z_lo: 2; z = z_hi * 2 + z_lo), core: 2. Of those that a mesh axis runs over, the one named last changes fastest.
Arguments:
- adjoint_in: float32 [4, 72, 512, 1024], P(None, None, 'gx', 'gy'), may hold values from -6 to 6
- courant_x: float32 [72, 512, 1024], P(None, 'gx', 'gy'), may hold values from -0.9 to 0.9
- courant_y: float32 [72, 512, 1024], P(None, 'gx', 'gy'), may hold values from -0.9 to 0.9
- mixing: float32 [71, 512, 1024], P(None, 'gx', 'gy'), may hold values from 0.05 to 5
- kernel_rows: bfloat16 [72, 524288], P(None, ('gx', 'gy')), may hold values from -6 to 6
- tracer_weights: bfloat16 [4, 524288], P(None, ('gx', 'gy')), may hold values from 0.25 to 1.5
- column_ids: int32 [524288], P(('gx', 'gy')), may hold values from 0 to 4095
- counts: int32 [128, 128], P(('gx', 'gy')), may hold values from 0 to 32, as said below
Outputs:
- adjoint_out: float32 [4, 72, 512, 1024], P(None, None, 'gx', 'gy')
- flux_gradient: float32 [4, 512, 1024], P(None, 'gx', 'gy')
The draws below stay inside these ranges and needn't reach their ends.
Inputs may be any that keep to these rules, and one draw needn't show every extreme that they name: `counts`: live slots from one device to another; 32 is reached by one receiving device from every sender. `column_ids`: column id in the receiving tile, longitude-major.
All inputs are finite; a program needn't handle non-finite values.
Results may differ from the reference program's by a relative error of at most 0.0003.
Values may be sent and summed in bfloat16 or wider, within the bound.
No kernel may reach another device: no remote copies, remote signals or barrier semaphores. Data moves between devices by JAX's collectives and lax.ppermute only.
A program may use at most 320 MiB of HBM per device.

```python
import math
import jax
import jax.numpy as jnp
from jax import lax

NTR = 4
LEV = 72
STEPS = 2
CX = 32
CY = 128
SLOTS = 32
NX = 512
NY = 1024
INTERFACES = 71
SOUNDINGS = 524288
N_GX = 16
N_GY = 8


def draw_counts(key, part):
    devices = N_GX * N_GY
    key_order, key_base, key_high = jax.random.split(key, 3)
    order = jax.random.permutation(key_order, devices)
    busy = order < max(1, devices // 8)
    full = order == 0
    base = jax.random.randint(key_base, (devices, devices), 0, SLOTS // 2 + 1)
    high = jax.random.randint(key_high, (devices, devices), SLOTS // 2, SLOTS + 1)
    result = jnp.where(busy[None, :], high, base)
    result = jnp.where(full[None, :], SLOTS, result)
    return result.astype(jnp.int32)


def set_ends(array, rng, low, high):
    dims = array.shape
    place = [jax.random.randint(jax.random.fold_in(rng, axis), (), 0, dims[axis]) for axis in range(len(dims))]
    array = array.at[tuple(place)].set(low)
    longest = dims.index(max(dims))
    place[longest] = (place[longest] + 1) % dims[longest]
    return array.at[tuple(place)].set(high)


def block_scale(rng, dims, pieces, smallest, top_value):
    gain = 1.0
    for position, parts in pieces:
        draws = jax.random.uniform(jax.random.fold_in(jax.random.fold_in(rng, 6), position), (parts,), jnp.float32, smallest / len(pieces), top_value / len(pieces))
        gain = gain * jnp.repeat(jnp.exp(draws), dims[position] // parts).reshape((-1,) + (1,) * (len(dims) - 1 - position))
    return gain


def bell_draw(own_key, extent, spread, limit, cuts=(), kind=jnp.bfloat16):
    gain = block_scale(own_key, extent, cuts, -0.22, 0.18) if cuts else 1.0
    values = jax.random.normal(own_key, extent, jnp.float32) * spread * gain
    return jnp.minimum(jnp.maximum(values, -limit), limit).astype(kind)


def setup_inputs(seed: int = 0) -> dict:
    key_of = jax.random.split(jax.random.key(seed), 9)
    return {
        "adjoint_in": bell_draw(key_of[0], (NTR, LEV, NX, NY), 1.0, 6.0, ((2, 16), (3, 8)), jnp.float32),
        "courant_x": jnp.clip(jax.random.uniform(key_of[1], (LEV, NX, NY), jnp.float32, -0.9, 0.9) * block_scale(key_of[1], (LEV, NX, NY), ((1, 16), (2, 8)), -0.4, 0.0), -0.9, 0.9),
        "courant_y": jnp.clip(jax.random.uniform(key_of[2], (LEV, NX, NY), jnp.float32, -0.9, 0.9) * block_scale(key_of[2], (LEV, NX, NY), ((1, 16), (2, 8)), -0.4, 0.0), -0.9, 0.9),
        "mixing": jnp.clip(jnp.exp(math.log(5.0) - 4.6051702 * jax.random.uniform(key_of[3], (INTERFACES, NX, NY), jnp.float32) ** block_scale(key_of[3], (INTERFACES, NX, NY), ((1, 16), (2, 8)), -0.2, 0.2)), 0.05, 5.0),
        "kernel_rows": bell_draw(key_of[4], (LEV, SOUNDINGS), 1.0, 6.0, ((1, 128),)),
        "tracer_weights": jnp.clip(0.25 + 1.25 * jax.random.uniform(key_of[5], (NTR, SOUNDINGS), jnp.float32) ** block_scale(key_of[5], (NTR, SOUNDINGS), ((1, 128),), -0.2, 0.2), 0.25, 1.5).astype(jnp.bfloat16),
        "column_ids": set_ends(jax.random.randint(key_of[6], (SOUNDINGS,), 0, CX * CY), jax.random.fold_in(key_of[6], 1), 0, (CX * CY) - 1).astype(jnp.int32),
        "counts": draw_counts(jax.random.fold_in(key_of[8], 71), 0),
    }


first_coef = (0.75, -0.15, 1.0 / 60.0)
second_coef = (1.5, -0.15, 1.0 / 90.0)
second_center = -49.0 / 18.0


def advect(padded, courant, axis, length):
    def piece(offset):
        return lax.slice_in_dim(padded, 3 + offset, 3 + offset + length, axis=axis)
    center = piece(0)
    slope = first_coef[0] * (piece(1) - piece(-1))
    curve = second_center * center + second_coef[0] * (piece(1) + piece(-1))
    for shift_k in (2, 3):
        slope = slope + first_coef[shift_k - 1] * (piece(shift_k) - piece(-shift_k))
        curve = curve + second_coef[shift_k - 1] * (piece(shift_k) + piece(-shift_k))
    return center + courant * slope + 0.5 * courant * courant * curve


def factor(mixing):
    levels = mixing.shape[0] + 1
    cps = []
    invs = []
    for level in range(levels):
        diag_part = jnp.ones_like(mixing[0])
        if level > 0:
            diag_part = diag_part + mixing[level - 1]
        if level < levels - 1:
            diag_part = diag_part + mixing[level]
        if level > 0:
            diag_part = diag_part - mixing[level - 1] * cps[level - 1] * (-1.0)
        inverse = 1.0 / diag_part
        invs.append(inverse)
        if level < levels - 1:
            cps.append(-mixing[level] * inverse)
    return cps, invs


def solve(field, mixing, cps, invs):
    levels = len(invs)
    carry = field[..., 0, :, :] * invs[0]
    forward = [carry]
    for level in range(1, levels):
        carry = (field[..., level, :, :] + mixing[level - 1] * carry) * invs[level]
        forward.append(carry)
    result = [None] * levels
    result[levels - 1] = forward[levels - 1]
    for level in range(levels - 2, -1, -1):
        result[level] = forward[level] - cps[level] * result[level + 1]
    return jnp.stack(result, axis=-3)


def reference(adjoint_in, courant_x, courant_y, mixing, kernel_rows, tracer_weights, column_ids, counts):
    devices = N_GX * N_GY
    total = devices * devices * SLOTS
    index = jnp.arange(total, dtype=jnp.int32)
    source = index // (devices * SLOTS)
    target = (index // SLOTS) % devices
    slot = index % SLOTS
    live = slot < counts[source, target]
    cell = column_ids[(target * devices + source) * SLOTS + slot]
    lon_cell = (target // N_GY) * CX + cell // CY
    lat_cell = (target % N_GY) * CY + cell % CY
    flat = (lon_cell * NY + lat_cell).astype(jnp.int32)
    live_rows = jnp.where(live[None, :], kernel_rows, jnp.zeros_like(kernel_rows)).astype(jnp.float32)
    cps, invs = factor(mixing)

    def one_tracer(inputs):
        weight_row, start = inputs
        values = live_rows * weight_row[None, :]
        forcing = jnp.zeros((LEV, NX * NY), jnp.float32).at[:, flat].add(values)
        state = start + forcing.reshape(LEV, NX, NY)
        gradient = jnp.zeros((NX, NY), jnp.float32)
        for step in range(STEPS):
            wrapped = jnp.concatenate([state[:, -3:], state, state[:, :3]], axis=1)
            zonal = advect(wrapped, courant_x, 1, NX)
            padded = jnp.pad(zonal, ((0, 0), (0, 0), (3, 3)))
            meridional = advect(padded, courant_y, 2, NY)
            state = solve(meridional, mixing, cps, invs)
            gradient = gradient + state[0]
        return state, gradient

    adjoint_out, flux_gradient = lax.map(one_tracer, (tracer_weights.astype(jnp.float32), adjoint_in))
    return adjoint_out, flux_gradient
```

```python
import jax
import jax.numpy as jnp
from jax import lax
from jax.experimental import pallas as pl
from jax.experimental.pallas import tpu as pltpu
from jax.sharding import PartitionSpec as P

STEPS = 2
LB = 8

D1, D2, D3 = 0.75, -0.15, 1.0 / 60.0
E1, E2, E3 = 1.5, -0.15, 1.0 / 90.0
E0 = -49.0 / 18.0

f32 = jnp.float32
bf16 = jnp.bfloat16


def swap_blocks(x, lane):
    upper = (lane & 64) != 0
    odd = (lane & 32) != 0
    y = [None] * 4
    for a in (0, 1):
        y[a] = jnp.where(upper, pltpu.roll(x[a + 2], 64, 1), x[a])
        y[a + 2] = jnp.where(upper, x[a + 2], pltpu.roll(x[a], 64, 1))
    z = [None] * 4
    for a in (0, 2):
        z[a] = jnp.where(odd, pltpu.roll(y[a + 1], 32, 1), y[a])
        z[a + 1] = jnp.where(odd, y[a + 1], pltpu.roll(y[a], 96, 1))
    return z


def split(value):
    hi = value.astype(bf16)
    return hi, (value - hi.astype(f32)).astype(bf16)


def pack_kernel(counts, rows, weights, out):
    lane = lax.broadcasted_iota(jnp.int32, (24, 128), 1)
    block = lane >> 5

    def group(g, _):
        lanes = pl.ds(pl.multiple_of(g * 128, 128), 128)
        limit = jnp.where(
            block < 2,
            jnp.where(block == 0, counts[0, 4 * g], counts[0, 4 * g + 1]),
            jnp.where(block == 2, counts[0, 4 * g + 2], counts[0, 4 * g + 3]),
        )
        live = (lane & 31) < limit
        parts = [jnp.where(live, rows[24 * q : 24 * q + 24, lanes].astype(f32), 0.0) for q in range(3)]
        parts.append(jnp.concatenate([weights[:, lanes].astype(f32), jnp.zeros((20, 128), f32)], axis=0))
        for i, piece in enumerate(swap_blocks(parts, lane)):
            out[4 * g + i] = piece.astype(bf16)
        return 0

    lax.fori_loop(0, out.shape[0] // 4, group, 0, unroll=2)


def factor_kernel(mixing, inv_out, q_out):
    levels = inv_out.shape[0]
    top = mixing[0]
    inv = 1.0 / (1.0 + top)
    q = top * inv
    inv_out[0] = inv
    q_out[0] = q

    def level(l, carry):
        below, q = carry
        above = mixing[l]
        inv = 1.0 / (1.0 + below + above - below * q)
        q = above * inv
        inv_out[l] = inv
        q_out[l] = q
        return above, q

    below, q = lax.fori_loop(1, levels - 1, level, (top, q))
    inv_out[levels - 1] = 1.0 / (1.0 + below - below * q)
    q_out[levels - 1] = jnp.zeros_like(q)


def forcing_kernel(got, code, adjoint, state, x_low, x_high, lhs):
    step = pl.program_id(0)
    lane = lax.broadcasted_iota(jnp.int32, (24, 128), 1)
    half = lhs.shape[0] // 2
    slots = lhs.shape[1]

    @pl.when(step == 0)
    def _():
        def group(g, _):
            lanes = pl.ds(pl.multiple_of(g * 128, 128), 128)
            parts = swap_blocks([got[4 * g + i].astype(f32) for i in range(4)], lane)
            for t in range(4):
                weight = parts[3][t : t + 1, :]
                for q in range(3):
                    hi, lo = split(parts[q] * weight)
                    row = 72 * t + 24 * q
                    lhs[row : row + 24, lanes] = hi
                    lhs[half + row : half + row + 24, lanes] = lo
            return 0

        lax.fori_loop(0, slots // 128, group, 0)

    chunk = min(1024, slots)
    one, zero = jnp.ones((), bf16), jnp.zeros((), bf16)
    results = []
    for pair in range(4):
        lon = step * 8 + 2 * pair
        total = None
        for k in range(slots // chunk):
            part = code[k * chunk : (k + 1) * chunk, :]
            placed = jnp.concatenate(
                [jnp.where(part == (lon + a).astype(f32).astype(bf16), one, zero) for a in range(2)], axis=1
            )
            product = jnp.dot(lhs[:, k * chunk : (k + 1) * chunk], placed, preferred_element_type=f32)
            total = product if total is None else total + product
        total = total[:half] + total[half:]
        for a in range(2):
            cell = adjoint[:, 2 * pair + a, :] + total[:, 128 * a : 128 * a + 128]
            state[:, 2 * pair + a, :] = cell

    @pl.when(step == 0)
    def _():
        low_edge(state, x_low)

    @pl.when(step == pl.num_programs(0) - 1)
    def _():
        high_edge(state, x_high)


def low_edge(state, out):
    out[0], out[1] = split(state[:, 0, :])
    out[2] = state[:, 1, :].astype(bf16)
    out[3] = state[:, 2, :].astype(bf16)


def high_edge(state, out):
    out[0], out[1] = split(state[:, 7, :])
    out[2] = state[:, 6, :].astype(bf16)
    out[3] = state[:, 5, :].astype(bf16)


def zonal_kernel(state, courant, left, right, zonal, to_left, to_right, pad):
    lane = lax.broadcasted_iota(jnp.int32, (8, 128), 1)
    group = lane >> 2
    for t in range(4):
        base = t * LB * 48
        for where, halo in ((0, left), (1, right)):
            near = halo[0, t].astype(f32) + halo[1, t].astype(f32)
            for k, value in enumerate((near, halo[2, t].astype(f32), halo[3, t].astype(f32))):
                row = base + (7 - k if where == 0 else 40 + k)
                pad[pl.ds(row, LB, stride=48), :] = value
        for l in range(LB):
            for r in range(4):
                pad[base + 48 * l + 8 + 8 * r : base + 48 * l + 16 + 8 * r, :] = state[t, l, 8 * r : 8 * r + 8, :]
    for r in range(4):
        lefts = jnp.zeros((8, 128), f32)
        rights = jnp.zeros((8, 128), f32)
        for l in range(LB):
            c = courant[l, 8 * r : 8 * r + 8, :]
            c2 = 0.5 * c * c
            for t in range(4):
                base = (t * LB + l) * 48 + 8 + 8 * r
                v = {k: pad[base + k : base + k + 8, :] for k in range(-3, 4)}
                out = stencil(v, c, c2)
                zonal[t, l, 8 * r : 8 * r + 8, :] = out
                i = t * LB + l
                mine = group == i
                lefts = jnp.where(mine, turn(out, 4 * i), lefts)
                rights = jnp.where(mine, turn(out, 4 * i + 3), rights)
        rest = (lane & 3) == 3
        for source, shift, dest in ((lefts, 3, to_left), (rights, 1, to_right)):
            hi = source.astype(bf16).astype(f32)
            dest[0, 8 * r : 8 * r + 8, :] = jnp.where(rest, pltpu.roll(source - hi, shift, 1), hi).astype(bf16)


def turn(value, shift):
    shift = shift % 128
    return value if shift == 0 else pltpu.roll(value, shift, 1)


def stencil(v, c, c2):
    slope = D1 * (v[1] - v[-1]) + D2 * (v[2] - v[-2]) + D3 * (v[3] - v[-3])
    curve = E0 * v[0] + E1 * (v[1] + v[-1]) + E2 * (v[2] + v[-2]) + E3 * (v[3] + v[-3])
    return v[0] + c * slope + c2 * curve


def column_kernel(first, zonal, courant, mixing, inv, q, left, right, *rest):
    if first:
        state, gradient, x_low, x_high = rest
    else:
        before, state, gradient = rest
    step = pl.program_id(0)
    levels = inv.shape[0]
    lane = lax.broadcasted_iota(jnp.int32, (8, 128), 1)
    third = (lane & 3) == 2
    zeroth = (lane & 3) == 0
    middle = lane < 64

    def block(b, carry):
        ml = left[b].astype(f32)
        ml = ml + jnp.where(third, pltpu.roll(ml, 127, 1), 0.0)
        mr = right[b].astype(f32)
        mr = mr + jnp.where(zeroth, pltpu.roll(mr, 125, 1), 0.0)
        for l in range(LB):
            level = b * LB + l
            c = courant[level]
            c2 = 0.5 * c * c
            m = mixing[jnp.maximum(level - 1, 0)]
            iv = inv[level]
            after = []
            for t in range(4):
                i = t * LB + l
                x = zonal[t, level]
                halo = jnp.where(middle, turn(mr, -4 * i), turn(ml, 125 - 4 * i))
                v = {0: x}
                for k in (1, 2, 3):
                    v[-k] = pltpu.roll(jnp.where(lane >= 128 - k, halo, x), k, 1)
                    v[k] = pltpu.roll(jnp.where(lane < k, halo, x), 128 - k, 1)
                y = stencil(v, c, c2)
                y = (y + m * carry[t]) * iv
                state[t, level] = y
                after.append(y)
            carry = tuple(after)
        return carry

    carry = tuple(jnp.zeros((8, 128), f32) for _ in range(4))
    carry = lax.fori_loop(0, levels // LB, block, carry)

    def back(j, carry):
        level = levels - 2 - j
        qq = q[level]
        after = []
        for t in range(4):
            y = state[t, level] + qq * carry[t]
            state[t, level] = y
            after.append(y)
        return tuple(after)

    carry = lax.fori_loop(0, levels - 1, back, carry, unroll=4)
    for t in range(4):
        gradient[t] = carry[t] if first else before[t] + carry[t]
    if first:

        @pl.when(step == 0)
        def _():
            for t in range(4):
                rows = slice(72 * t, 72 * t + 72)
                x_low[0, rows], x_low[1, rows] = split(state[t, :, 0, :])
                x_low[2, rows] = state[t, :, 1, :].astype(bf16)
                x_low[3, rows] = state[t, :, 2, :].astype(bf16)

        @pl.when(step == pl.num_programs(0) - 1)
        def _():
            for t in range(4):
                rows = slice(72 * t, 72 * t + 72)
                x_high[0, rows], x_high[1, rows] = split(state[t, :, 7, :])
                x_high[2, rows] = state[t, :, 6, :].astype(bf16)
                x_high[3, rows] = state[t, :, 5, :].astype(bf16)


def cost(flops, size):
    return pl.CostEstimate(flops=flops, bytes_accessed=size, transcendentals=0)


def params(mib):
    return pltpu.CompilerParams(vmem_limit_bytes=mib * 2**20)


def shape(dims, kind=f32):
    return jax.ShapeDtypeStruct(dims, kind)


def whole(dims):
    return pl.BlockSpec(dims, lambda i: (0,) * len(dims))


def shift(value, axis, closed, forward):
    count = lax.axis_size(axis)
    ends = count if closed else count - 1
    pairs = [(i, (i + 1) % count) for i in range(ends)]
    if not forward:
        pairs = [(b, a) for a, b in pairs]
    return lax.ppermute(value, axis, pairs)


def local(adjoint_in, courant_x, courant_y, mixing, kernel_rows, tracer_weights, column_ids, counts):
    tracers, levels, lons, lats = adjoint_in.shape
    devices = lax.axis_size(("gx", "gy"))
    slots = kernel_rows.shape[1]
    fields = tracers * levels
    size = fields * lons * lats * 4

    packed = pl.pallas_call(
        pack_kernel,
        out_shape=shape((devices, 24, 128), bf16),
        in_specs=[pl.BlockSpec(memory_space=pltpu.SMEM), pl.BlockSpec(), pl.BlockSpec()],
        compiler_params=params(16),
        name="pack",
    )(counts, kernel_rows, tracer_weights)
    got = lax.all_to_all(packed, ("gx", "gy"), split_axis=0, concat_axis=0, tiled=True)

    inv, q = pl.pallas_call(
        factor_kernel,
        out_shape=[shape((levels, lons, lats))] * 2,
        compiler_params=params(16),
        cost_estimate=cost(30 * levels * lons * lats, 3 * levels * lons * lats * 4),
        name="factor",
    )(mixing)
    lat_range = jnp.arange(lats, dtype=jnp.int32)
    code = jnp.where(
        (column_ids % lats)[:, None] == lat_range[None, :], (column_ids // lats)[:, None], -1
    ).astype(bf16)

    edge = shape((4, fields, lats), bf16)
    state, x_low, x_high = pl.pallas_call(
        forcing_kernel,
        grid=(lons // 8,),
        in_specs=[
            whole((devices, 24, 128)),
            whole((slots, lats)),
            pl.BlockSpec((fields, 8, lats), lambda i: (0, i, 0)),
        ],
        out_specs=[
            pl.BlockSpec((fields, 8, lats), lambda i: (0, i, 0)),
            whole((4, fields, lats)),
            whole((4, fields, lats)),
        ],
        out_shape=[shape((fields, lons, lats)), edge, edge],
        scratch_shapes=[pltpu.VMEM((2 * fields, slots), bf16)],
        compiler_params=params(40),
        cost_estimate=cost(4 * fields * slots * lons * lats, 2 * size),
        name="forcing",
    )(got, code, adjoint_in.reshape(fields, lons, lats))

    for step in range(STEPS):
        from_left = shift(x_high, "gx", True, True)
        from_right = shift(x_low, "gx", True, False)
        blocks = levels // LB
        halo_spec = pl.BlockSpec((4, tracers, LB, lats), lambda b: (0, 0, b, 0))
        field_spec = pl.BlockSpec((tracers, LB, lons, lats), lambda b: (0, b, 0, 0))
        note_spec = pl.BlockSpec((1, lons, 128), lambda b: (b, 0, 0))
        zonal, to_left, to_right = pl.pallas_call(
            zonal_kernel,
            grid=(blocks,),
            in_specs=[
                field_spec,
                pl.BlockSpec((LB, lons, lats), lambda b: (b, 0, 0)),
                halo_spec,
                halo_spec,
            ],
            out_specs=[field_spec, note_spec, note_spec],
            out_shape=[
                shape((tracers, levels, lons, lats)),
                shape((blocks, lons, 128), bf16),
                shape((blocks, lons, 128), bf16),
            ],
            scratch_shapes=[pltpu.VMEM((tracers * LB * 48, lats), f32)],
            compiler_params=params(24),
            cost_estimate=cost(20 * size // 4, 2 * size),
            name="zonal",
        )(
            state.reshape(tracers, levels, lons, lats),
            courant_x,
            from_left.reshape(4, tracers, levels, lats),
            from_right.reshape(4, tracers, levels, lats),
        )
        y_left = shift(to_right, "gy", False, True)
        y_right = shift(to_left, "gy", False, False)
        first = step == 0
        field_spec = pl.BlockSpec((tracers, levels, 8, lats), lambda r: (0, 0, r, 0))
        level_spec = pl.BlockSpec((levels, 8, lats), lambda r: (0, r, 0))
        note_spec = pl.BlockSpec((blocks, 8, 128), lambda r: (0, r, 0))
        gradient_spec = pl.BlockSpec((tracers, 8, lats), lambda r: (0, r, 0))
        mixing_spec = pl.BlockSpec((levels - 1, 8, lats), lambda r: (0, r, 0))
        operands = [zonal, courant_y, mixing, inv, q, y_left, y_right]
        in_specs = [field_spec, level_spec, mixing_spec, level_spec, level_spec, note_spec, note_spec]
        out_specs = [field_spec, gradient_spec]
        out_shape = [shape((tracers, levels, lons, lats)), shape((tracers, lons, lats))]
        if first:
            out_specs += [whole((4, fields, lats))] * 2
            out_shape += [edge, edge]
        else:
            operands.append(gradient)
            in_specs.append(gradient_spec)

        def kernel(*refs, first=first):
            column_kernel(first, *refs)

        out = pl.pallas_call(
            kernel,
            grid=(lons // 8,),
            in_specs=in_specs,
            out_specs=out_specs,
            out_shape=out_shape,
            compiler_params=params(32),
            cost_estimate=cost(40 * size // 4, 2 * size),
            name="column",
        )(*operands)
        if first:
            state, gradient, x_low, x_high = out
        else:
            state, gradient = out
    return state, gradient


def solution(mesh):
    in_specs = (
        P(None, None, "gx", "gy"),
        P(None, "gx", "gy"),
        P(None, "gx", "gy"),
        P(None, "gx", "gy"),
        P(None, ("gx", "gy")),
        P(None, ("gx", "gy")),
        P(("gx", "gy")),
        P(("gx", "gy"), None),
    )
    out_specs = (P(None, None, "gx", "gy"), P(None, "gx", "gy"))
    return jax.shard_map(local, mesh=mesh, in_specs=in_specs, out_specs=out_specs, check_vma=False)
```

```python
import jax
import jax.numpy as jnp
import numpy as np
from jax import lax
from jax.experimental import pallas as pl
from jax.experimental.pallas import tpu as pltpu
from jax.sharding import PartitionSpec as P

STEPS = 2
LB = 8
CHUNK = 1024

D1, D2, D3 = 0.75, -0.15, 1.0 / 60.0
E1, E2, E3 = 1.5, -0.15, 1.0 / 90.0
E0 = -49.0 / 18.0

f32 = jnp.float32
bf16 = jnp.bfloat16


def fill_swap(table):
    row = lax.broadcasted_iota(jnp.int32, table.shape, 0)
    col = lax.broadcasted_iota(jnp.int32, table.shape, 1)
    want = ((col >> 5) & 3) * 128 + (col >> 7) * 32 + (col & 31)
    table[...] = jnp.where(row == want, 1.0, 0.0).astype(bf16)


def split(value):
    hi = value.astype(bf16)
    return hi, (value - hi.astype(f32)).astype(bf16)


def pack_kernel(counts, rows, weights, out, swap):
    step = pl.program_id(0)
    groups = rows.shape[1] // 128

    @pl.when(step == 0)
    def _():
        fill_swap(swap)

    lane = lax.broadcasted_iota(jnp.int32, (24, 128), 1)
    block = lane >> 5
    columns = [[] for _ in range(4)]
    for g in range(groups):
        lanes = slice(g * 128, g * 128 + 128)
        first = 4 * (step * groups + g)
        limit = jnp.where(
            block < 2,
            jnp.where(block == 0, counts[0, first], counts[0, first + 1]),
            jnp.where(block == 2, counts[0, first + 2], counts[0, first + 3]),
        )
        live = (lane & 31) < limit
        for q in range(3):
            columns[q].append(jnp.where(live, rows[24 * q : 24 * q + 24, lanes].astype(f32), 0.0))
        columns[3].append(jnp.concatenate([weights[:, lanes].astype(f32), jnp.zeros((20, 128), f32)], axis=0))
    wide = jnp.concatenate([jnp.concatenate(c, axis=0).astype(bf16) for c in columns], axis=1)
    moved = jnp.dot(wide, swap[...], preferred_element_type=f32)
    for g in range(groups):
        for i in range(4):
            out[4 * g + i] = moved[24 * g : 24 * g + 24, 128 * i : 128 * i + 128].astype(bf16)


def factor_kernel(mixing, inv_out, q_out):
    levels = inv_out.shape[0]
    top = mixing[0]
    inv = 1.0 / (1.0 + top)
    q = top * inv
    inv_out[0] = inv
    q_out[0] = q

    def level(l, carry):
        below, q = carry
        above = mixing[l]
        inv = 1.0 / (1.0 + below + above - below * q)
        q = above * inv
        inv_out[l] = inv
        q_out[l] = q
        return above, q

    below, q = lax.fori_loop(1, levels - 1, level, (top, q))
    inv_out[levels - 1] = 1.0 / (1.0 + below - below * q)
    q_out[levels - 1] = jnp.zeros_like(q)


def rank_kernel(bins, code, starts):
    piece = 256
    lane = lax.broadcasted_iota(jnp.int32, (piece, 128), 1)
    lane_f = lane.astype(f32)
    upto = (lax.broadcasted_iota(jnp.int32, (piece, piece), 1) <= lax.broadcasted_iota(jnp.int32, (piece, piece), 0))
    upto = jnp.where(upto, 1.0, 0.0).astype(bf16)
    row2 = lax.broadcasted_iota(jnp.int32, (256, 256), 0)
    col2 = lax.broadcasted_iota(jnp.int32, (256, 256), 1)
    spread = jnp.where((row2 >> 7) == (col2 >> 7), 1.0, 0.0).astype(bf16)
    ones = jnp.ones((8, CHUNK), bf16)
    for h in range(bins.shape[0] // CHUNK):
        own = bins[h * CHUNK : (h + 1) * CHUNK, :].astype(f32)
        wide = lax.broadcasted_iota(jnp.int32, own.shape, 1).astype(f32)
        below = jnp.where(own < wide, 1.0, 0.0).astype(bf16)
        start = jnp.dot(ones, below, preferred_element_type=f32)
        starts[8 * h : 8 * h + 8, :] = start.astype(jnp.int32)
        running = start[0:1, :] - 1.0
        for p in range(CHUNK // piece):
            at = slice(p * piece, p * piece + piece)
            mine = own[at] == lane_f
            one_hot = jnp.where(mine, 1.0, 0.0)
            place = jnp.dot(upto, one_hot.astype(bf16), preferred_element_type=f32) + running
            running = place[piece - 1 : piece, :]
            place = jnp.where(mine, place, 0.0)
            high = jnp.floor(place * (1.0 / 128.0))
            low = place - 128.0 * high
            both = jnp.dot(
                jnp.concatenate([high.astype(bf16), low.astype(bf16)], axis=1), spread, preferred_element_type=f32
            )
            found = jnp.where(both[:, 128:] == lane_f, both[:, :128], -1.0)
            code[h * CHUNK + p * piece : h * CHUNK + (p + 1) * piece, :] = found.astype(bf16)


def order_kernel(got, ids, code, lhs, places, swap, raw):
    half = lhs.shape[0] // 2
    slots = lhs.shape[1]
    fill_swap(swap)
    batch = 8
    for first in range(0, slots // 128, batch):
        wide = jnp.concatenate(
            [
                jnp.concatenate([got[4 * (first + g) + i].astype(f32) for g in range(batch)], axis=0).astype(bf16)
                for i in range(4)
            ],
            axis=1,
        )
        moved = jnp.dot(wide, swap[...], preferred_element_type=f32)
        for g in range(batch):
            lanes = slice((first + g) * 128, (first + g) * 128 + 128)
            for q in range(4):
                count = 24 if q < 3 else 8
                raw[24 * q : 24 * q + count, lanes] = moved[24 * g : 24 * g + count, 128 * q : 128 * q + 128]
    cells = ids[...]
    raw[76:77, :] = (cells & 127).astype(f32)
    raw[77:78, :] = (cells >> 7).astype(f32)
    one, zero = jnp.ones((), bf16), jnp.zeros((), bf16)
    for h in range(slots // CHUNK):
        block = raw[:, h * CHUNK : (h + 1) * CHUNK].astype(bf16)
        part = code[h * CHUNK : (h + 1) * CHUNK, :]
        for p in range(CHUNK // 256):
            one_hot = jnp.concatenate(
                [jnp.where(part == jnp.asarray(2 * p + a, bf16), one, zero) for a in range(2)], axis=1
            )
            done = jnp.dot(block, one_hot, preferred_element_type=f32)
            lanes = slice(h * CHUNK + p * 256, h * CHUNK + (p + 1) * 256)
            places[:, lanes] = done[72:80, :]
            for t in range(4):
                hi, lo = split(done[:72] * done[72 + t : 73 + t, :])
                lhs[72 * t : 72 * t + 72, lanes] = hi
                lhs[half + 72 * t : half + 72 * t + 72, lanes] = lo


def forcing_kernel(starts, lhs, places, adjoint, state, x_low, x_high, total):
    step = pl.program_id(0)
    half = lhs.shape[0] // 2
    chunks = lhs.shape[1] // CHUNK
    row = lax.broadcasted_iota(jnp.int32, (128, 256), 0).astype(f32)

    def placed(at, lon):
        lat = places[4:5, pl.ds(at, 256)]
        slot_lon = places[5:6, pl.ds(at, 256)]
        return jnp.concatenate(
            [
                jnp.where(jnp.where(slot_lon == (lon + a).astype(f32), lat, -1.0) == row, 1.0, 0.0).astype(bf16)
                for a in range(2)
            ],
            axis=0,
        )

    def product(at, lon):
        return lax.dot_general(
            lhs[:, pl.ds(at, 256)], placed(at, lon), (((1,), (1,)), ((), ())), preferred_element_type=f32
        )

    for pair in range(4):
        lon = step * 8 + 2 * pair
        number = step * 4 + pair
        result = None
        limits = []
        for h in range(chunks):
            low = starts[8 * h, number]
            high = starts[8 * h, number + 1]
            first = jnp.minimum(low >> 7, CHUNK // 128 - 2)
            tiles = (high + 127) >> 7
            limits.append((first, tiles))
            at = pl.multiple_of(h * CHUNK + first * 128, 128)
            piece = product(at, lon)
            result = piece if result is None else result + piece
        total[...] = result
        for h, (first, tiles) in enumerate(limits):

            def more(j, _, h=h, first=first, lon=lon):
                at = first + 2 + 2 * j
                start = jnp.minimum(at, CHUNK // 128 - 2)
                fresh = lax.broadcasted_iota(jnp.int32, (1, 256), 1) >= (at - start) * 128
                base = pl.multiple_of(h * CHUNK + start * 128, 128)
                one_hot = jnp.where(fresh, placed(base, lon).astype(f32), 0.0).astype(bf16)
                total[...] += lax.dot_general(
                    lhs[:, pl.ds(base, 256)], one_hot, (((1,), (1,)), ((), ())), preferred_element_type=f32
                )
                return 0

            lax.fori_loop(0, jnp.maximum(tiles - first - 1, 0) >> 1, more, 0)
        for a in range(2):
            lanes = slice(128 * a, 128 * a + 128)
            state[:, 2 * pair + a, :] = adjoint[:, 2 * pair + a, :] + (total[:half, lanes] + total[half:, lanes])

    @pl.when(step == 0)
    def _():
        low_edge(state, x_low)

    @pl.when(step == pl.num_programs(0) - 1)
    def _():
        high_edge(state, x_high)


def low_edge(state, out):
    out[0], out[1] = split(state[:, 0, :])
    out[2] = state[:, 1, :].astype(bf16)
    out[3] = state[:, 2, :].astype(bf16)


def high_edge(state, out):
    out[0], out[1] = split(state[:, 7, :])
    out[2] = state[:, 6, :].astype(bf16)
    out[3] = state[:, 5, :].astype(bf16)


def zonal_kernel(state, courant, left, right, spread, zonal, to_left, to_right, pad, halves):
    lane = lax.broadcasted_iota(jnp.int32, (32, 128), 1)
    group = lane >> 2
    for t in range(4):
        base = t * LB * 48
        for where, halo in ((0, left), (1, right)):
            near = halo[0, t].astype(f32) + halo[1, t].astype(f32)
            for k, value in enumerate((near, halo[2, t].astype(f32), halo[3, t].astype(f32))):
                row = base + (7 - k if where == 0 else 40 + k)
                pad[pl.ds(row, LB, stride=48), :] = value
        for l in range(LB):
            pad[base + 48 * l + 8 : base + 48 * l + 40, :] = state[t, l]
    notes = [jnp.zeros((32, 128), f32)] * 2
    for t in range(4):
        for l in range(LB):
            c = courant[l]
            base = (t * LB + l) * 48 + 8
            out = stencil({k: pad[base + k : base + k + 32, :] for k in range(-3, 4)}, c, 0.5 * c * c)
            zonal[t, l] = out
            i = t * LB + l
            at = slice(32 * i, 32 * i + 32)
            halves[at, 0:128], halves[at, 128:256] = split(out)
        at = slice(32 * LB * t, 32 * LB * (t + 1))
        edges = jnp.dot(halves[at, :], spread[...], preferred_element_type=f32)
        for l in range(LB):
            mine = group == t * LB + l
            rows = slice(32 * l, 32 * l + 32)
            notes = [jnp.where(mine, edges[rows, 128 * n : 128 * n + 128], notes[n]) for n in range(2)]
    to_left[0] = notes[0].astype(bf16)
    to_right[0] = notes[1].astype(bf16)


def stencil(v, c, c2):
    slope = D1 * (v[1] - v[-1]) + D2 * (v[2] - v[-2]) + D3 * (v[3] - v[-3])
    curve = E0 * v[0] + E1 * (v[1] + v[-1]) + E2 * (v[2] + v[-2]) + E3 * (v[3] + v[-3])
    return v[0] + c * slope + c2 * curve


def column_kernel(first, zonal, courant, mixing, inv, q, left, right, weights, *rest):
    lhs = rest[-1]
    if first:
        state, gradient, x_low, x_high = rest[:-1]
    else:
        before, state, gradient = rest[:-1]
    step = pl.program_id(0)
    levels = inv.shape[0]
    rows = 32
    lane = lax.broadcasted_iota(jnp.int32, (rows, 128), 1)
    row = lax.broadcasted_iota(jnp.int32, (rows, 128), 0)
    owner = ((lane >> 2) - (row >> 3) * LB).astype(f32).astype(bf16)
    zero = jnp.zeros((), bf16)
    carry = None
    for b in range(levels // LB):
        notes = [jnp.concatenate([side[b].astype(f32)] * 4, axis=0).astype(bf16) for side in (left, right)]
        for l in range(LB):
            level = b * LB + l
            at = slice(level * rows, level * rows + rows)
            hi, lo = split(zonal[:, level].reshape(rows, 128))
            lhs[at, 0:128] = hi
            lhs[at, 128:256] = lo
            mine = owner == jnp.asarray(l, bf16)
            lhs[at, 256:384] = jnp.where(mine, notes[0], zero)
            lhs[at, 384:512] = jnp.where(mine, notes[1], zero)
        both = jnp.dot(
            lhs[b * LB * rows : (b + 1) * LB * rows, :], weights[...], preferred_element_type=f32
        )
        for l in range(LB):
            level = b * LB + l
            c = courant[level]
            c1 = c * (1.0 / 60.0)
            c2 = c * c * (1.0 / 360.0)
            part = both[l * rows : l * rows + rows].reshape(4, 8, 256)
            y = zonal[:, level] + c1 * part[:, :, :128] + c2 * part[:, :, 128:]
            if level > 0:
                y = y + mixing[level - 1] * carry
            carry = y * inv[level]
            state[:, level] = carry

    def back(j, carry):
        level = levels - 2 - j
        carry = state[:, level] + q[level] * carry
        state[:, level] = carry
        return carry

    carry = lax.fori_loop(0, levels - 1, back, carry, unroll=8)
    gradient[...] = carry if first else before[...] + carry
    if first:

        @pl.when(step == 0)
        def _():
            for t in range(4):
                rows = slice(72 * t, 72 * t + 72)
                x_low[0, rows], x_low[1, rows] = split(state[t, :, 0, :])
                x_low[2, rows] = state[t, :, 1, :].astype(bf16)
                x_low[3, rows] = state[t, :, 2, :].astype(bf16)

        @pl.when(step == pl.num_programs(0) - 1)
        def _():
            for t in range(4):
                rows = slice(72 * t, 72 * t + 72)
                x_high[0, rows], x_high[1, rows] = split(state[t, :, 7, :])
                x_high[2, rows] = state[t, :, 6, :].astype(bf16)
                x_high[3, rows] = state[t, :, 5, :].astype(bf16)


def edge_weights():
    table = np.zeros((256, 256), np.float32)
    for lane in range(128):
        part = lane % 4
        table[(128, part)[part < 3], lane] = 1
        table[(255, 125 + part)[part < 3], 128 + lane] = 1
    return table


def lat_weights():
    first = {1: 45, 2: -9, 3: 1}
    second = {0: -490, 1: 270, 2: -27, 3: 2}
    table = np.zeros((512, 256), np.float32)

    def fill(row, place):
        for out in range(128):
            k = place - out
            if abs(k) <= 3:
                table[row, out] = first.get(abs(k), 0) * (1 if k > 0 else -1)
                table[row, 128 + out] = second[abs(k)]

    for lane in range(128):
        fill(lane, lane)
        fill(128 + lane, lane)
        fill(256 + lane, (-3, -2, -1, -1)[lane % 4])
        fill(384 + lane, (128, 129, 130, 128)[lane % 4])
    return table


def cost(flops, size):
    return pl.CostEstimate(flops=flops, bytes_accessed=size, transcendentals=0)


def params(mib):
    return pltpu.CompilerParams(vmem_limit_bytes=mib * 2**20)


def shape(dims, kind=f32):
    return jax.ShapeDtypeStruct(dims, kind)


def whole(dims):
    return pl.BlockSpec(dims, lambda i: (0,) * len(dims))


def shift(value, axis, closed, forward):
    count = lax.axis_size(axis)
    ends = count if closed else count - 1
    pairs = [(i, (i + 1) % count) for i in range(ends)]
    if not forward:
        pairs = [(b, a) for a, b in pairs]
    return lax.ppermute(value, axis, pairs)


def local(adjoint_in, courant_x, courant_y, mixing, kernel_rows, tracer_weights, column_ids, counts):
    tracers, levels, lons, lats = adjoint_in.shape
    devices = lax.axis_size(("gx", "gy"))
    slots = kernel_rows.shape[1]
    fields = tracers * levels
    size = fields * lons * lats * 4

    packed = pl.pallas_call(
        pack_kernel,
        grid=(8,),
        in_specs=[
            pl.BlockSpec(memory_space=pltpu.SMEM),
            pl.BlockSpec((levels, slots // 8), lambda i: (0, i)),
            pl.BlockSpec((tracers, slots // 8), lambda i: (0, i)),
        ],
        out_specs=pl.BlockSpec((devices // 8, 24, 128), lambda i: (i, 0, 0)),
        out_shape=shape((devices, 24, 128), bf16),
        scratch_shapes=[pltpu.VMEM((512, 512), bf16)],
        compiler_params=params(60),
        name="pack",
    )(counts, kernel_rows, tracer_weights)
    got = lax.all_to_all(packed, ("gx", "gy"), split_axis=0, concat_axis=0, tiled=True)

    inv, q = pl.pallas_call(
        factor_kernel,
        out_shape=[shape((levels, lons, lats))] * 2,
        compiler_params=params(16),
        cost_estimate=cost(30 * levels * lons * lats, 3 * levels * lons * lats * 4),
        name="factor",
    )(mixing)
    bins = jnp.broadcast_to((column_ids // (2 * lats)).astype(bf16)[:, None], (slots, 128))
    code, starts = pl.pallas_call(
        rank_kernel,
        out_shape=[shape((slots, 128), bf16), shape((8 * (slots // CHUNK), 128), jnp.int32)],
        compiler_params=params(16),
        cost_estimate=cost(10**9, 2 * 10**6),
        name="rank",
    )(bins)
    lhs, places = pl.pallas_call(
        order_kernel,
        out_shape=[shape((2 * fields, slots), bf16), shape((8, slots))],
        scratch_shapes=[pltpu.VMEM((512, 512), bf16), pltpu.VMEM((80, slots), f32)],
        compiler_params=params(24),
        cost_estimate=cost(10**9, 8 * 10**6),
        name="order",
    )(got, column_ids.reshape(1, slots), code)

    edge = shape((4, fields, lats), bf16)
    state, x_low, x_high = pl.pallas_call(
        forcing_kernel,
        grid=(lons // 8,),
        in_specs=[
            pl.BlockSpec(memory_space=pltpu.SMEM),
            whole((2 * fields, slots)),
            whole((8, slots)),
            pl.BlockSpec((fields, 8, lats), lambda i: (0, i, 0)),
        ],
        out_specs=[
            pl.BlockSpec((fields, 8, lats), lambda i: (0, i, 0)),
            whole((4, fields, lats)),
            whole((4, fields, lats)),
        ],
        out_shape=[shape((fields, lons, lats)), edge, edge],
        scratch_shapes=[pltpu.VMEM((2 * fields, 2 * lats), f32)],
        compiler_params=params(32),
        cost_estimate=cost(10**10, 2 * size),
        name="forcing",
    )(starts, lhs, places, adjoint_in.reshape(fields, lons, lats))

    for step in range(STEPS):
        from_left = shift(x_high, "gx", True, True)
        from_right = shift(x_low, "gx", True, False)
        blocks = levels // LB
        halo_spec = pl.BlockSpec((4, tracers, LB, lats), lambda b: (0, 0, b, 0))
        field_spec = pl.BlockSpec((tracers, LB, lons, lats), lambda b: (0, b, 0, 0))
        note_spec = pl.BlockSpec((1, lons, 128), lambda b: (b, 0, 0))
        zonal, to_left, to_right = pl.pallas_call(
            zonal_kernel,
            grid=(blocks,),
            in_specs=[
                field_spec,
                pl.BlockSpec((LB, lons, lats), lambda b: (b, 0, 0)),
                halo_spec,
                halo_spec,
                whole((256, 256)),
            ],
            out_specs=[field_spec, note_spec, note_spec],
            out_shape=[
                shape((tracers, levels, lons, lats)),
                shape((blocks, lons, 128), bf16),
                shape((blocks, lons, 128), bf16),
            ],
            scratch_shapes=[
                pltpu.VMEM((tracers * LB * 48, lats), f32),
                pltpu.VMEM((tracers * LB * lons, 2 * lats), bf16),
            ],
            compiler_params=params(24),
            cost_estimate=cost(20 * size // 4, 2 * size),
            name="zonal",
        )(
            state.reshape(tracers, levels, lons, lats),
            courant_x,
            from_left.reshape(4, tracers, levels, lats),
            from_right.reshape(4, tracers, levels, lats),
            jnp.asarray(edge_weights(), bf16),
        )
        y_left = shift(to_right, "gy", False, True)
        y_right = shift(to_left, "gy", False, False)
        first = step == 0
        field_spec = pl.BlockSpec((tracers, levels, 8, lats), lambda r: (0, 0, r, 0))
        level_spec = pl.BlockSpec((levels, 8, lats), lambda r: (0, r, 0))
        note_spec = pl.BlockSpec((blocks, 8, 128), lambda r: (0, r, 0))
        gradient_spec = pl.BlockSpec((tracers, 8, lats), lambda r: (0, r, 0))
        mixing_spec = pl.BlockSpec((levels - 1, 8, lats), lambda r: (0, r, 0))
        operands = [zonal, courant_y, mixing, inv, q, y_left, y_right, jnp.asarray(lat_weights(), bf16)]
        in_specs = [field_spec, level_spec, mixing_spec, level_spec, level_spec, note_spec, note_spec, whole((512, 256))]
        out_specs = [field_spec, gradient_spec]
        out_shape = [shape((tracers, levels, lons, lats)), shape((tracers, lons, lats))]
        if first:
            out_specs += [whole((4, fields, lats))] * 2
            out_shape += [edge, edge]
        else:
            operands.append(gradient)
            in_specs.append(gradient_spec)

        def kernel(*refs, first=first):
            column_kernel(first, *refs)

        out = pl.pallas_call(
            kernel,
            grid=(lons // 8,),
            in_specs=in_specs,
            out_specs=out_specs,
            out_shape=out_shape,
            scratch_shapes=[pltpu.VMEM((levels * tracers * 8, 512), bf16)],
            compiler_params=params(32),
            cost_estimate=cost(40 * size // 4, 2 * size),
            name="column",
        )(*operands)
        if first:
            state, gradient, x_low, x_high = out
        else:
            state, gradient = out
    return state, gradient


def solution(mesh):
    in_specs = (
        P(None, None, "gx", "gy"),
        P(None, "gx", "gy"),
        P(None, "gx", "gy"),
        P(None, "gx", "gy"),
        P(None, ("gx", "gy")),
        P(None, ("gx", "gy")),
        P(("gx", "gy")),
        P(("gx", "gy"), None),
    )
    out_specs = (P(None, None, "gx", "gy"), P(None, "gx", "gy"))
    return jax.shard_map(local, mesh=mesh, in_specs=in_specs, out_specs=out_specs, check_vma=False)
```

```python
import jax
import jax.numpy as jnp
import numpy as np
from jax import lax
from jax.experimental import pallas as pl
from jax.experimental.pallas import tpu as pltpu
from jax.sharding import PartitionSpec as P

STEPS = 2
LB = 8
CHUNK = 1024

D1, D2, D3 = 0.75, -0.15, 1.0 / 60.0
E1, E2, E3 = 1.5, -0.15, 1.0 / 90.0
E0 = -49.0 / 18.0

f32 = jnp.float32
bf16 = jnp.bfloat16


def fill_swap(table):
    row = lax.broadcasted_iota(jnp.int32, table.shape, 0)
    col = lax.broadcasted_iota(jnp.int32, table.shape, 1)
    want = ((col >> 5) & 3) * 128 + (col >> 7) * 32 + (col & 31)
    table[...] = jnp.where(row == want, 1.0, 0.0).astype(bf16)


def split(value):
    hi = value.astype(bf16)
    return hi, (value - hi.astype(f32)).astype(bf16)


def pack_kernel(counts, rows, weights, out, swap):
    step = pl.program_id(0)
    groups = rows.shape[1] // 128

    @pl.when(step == 0)
    def _():
        fill_swap(swap)

    lane = lax.broadcasted_iota(jnp.int32, (24, 128), 1)
    block = lane >> 5
    columns = [[] for _ in range(4)]
    for g in range(groups):
        lanes = slice(g * 128, g * 128 + 128)
        first = 4 * (step * groups + g)
        limit = jnp.where(
            block < 2,
            jnp.where(block == 0, counts[0, first], counts[0, first + 1]),
            jnp.where(block == 2, counts[0, first + 2], counts[0, first + 3]),
        )
        live = (lane & 31) < limit
        for q in range(3):
            columns[q].append(jnp.where(live, rows[24 * q : 24 * q + 24, lanes].astype(f32), 0.0))
        columns[3].append(jnp.concatenate([weights[:, lanes].astype(f32), jnp.zeros((20, 128), f32)], axis=0))
    wide = jnp.concatenate([jnp.concatenate(c, axis=0).astype(bf16) for c in columns], axis=1)
    moved = jnp.dot(wide, swap[...], preferred_element_type=f32)
    for g in range(groups):
        for i in range(4):
            out[4 * g + i] = moved[24 * g : 24 * g + 24, 128 * i : 128 * i + 128].astype(bf16)


def factor_kernel(mixing, inv_out, q_out):
    levels = inv_out.shape[0]
    top = mixing[0]
    inv = 1.0 / (1.0 + top)
    q = top * inv
    inv_out[0] = inv
    q_out[0] = q

    def level(l, carry):
        below, q = carry
        above = mixing[l]
        inv = 1.0 / (1.0 + below + above - below * q)
        q = above * inv
        inv_out[l] = inv
        q_out[l] = q
        return above, q

    below, q = lax.fori_loop(1, levels - 1, level, (top, q))
    inv_out[levels - 1] = 1.0 / (1.0 + below - below * q)
    q_out[levels - 1] = jnp.zeros_like(q)


def rank_kernel(bins, code, starts):
    piece = 256
    lane = lax.broadcasted_iota(jnp.int32, (piece, 128), 1)
    lane_f = lane.astype(f32)
    upto = (lax.broadcasted_iota(jnp.int32, (piece, piece), 1) <= lax.broadcasted_iota(jnp.int32, (piece, piece), 0))
    upto = jnp.where(upto, 1.0, 0.0).astype(bf16)
    row2 = lax.broadcasted_iota(jnp.int32, (256, 256), 0)
    col2 = lax.broadcasted_iota(jnp.int32, (256, 256), 1)
    spread = jnp.where((row2 >> 7) == (col2 >> 7), 1.0, 0.0).astype(bf16)
    ones = jnp.ones((8, CHUNK), bf16)
    for h in range(bins.shape[0] // CHUNK):
        own = bins[h * CHUNK : (h + 1) * CHUNK, :].astype(f32)
        wide = lax.broadcasted_iota(jnp.int32, own.shape, 1).astype(f32)
        below = jnp.where(own < wide, 1.0, 0.0).astype(bf16)
        start = jnp.dot(ones, below, preferred_element_type=f32)
        starts[8 * h : 8 * h + 8, :] = start.astype(jnp.int32)
        running = start[0:1, :] - 1.0
        for p in range(CHUNK // piece):
            at = slice(p * piece, p * piece + piece)
            mine = own[at] == lane_f
            one_hot = jnp.where(mine, 1.0, 0.0)
            place = jnp.dot(upto, one_hot.astype(bf16), preferred_element_type=f32) + running
            running = place[piece - 1 : piece, :]
            place = jnp.where(mine, place, 0.0)
            high = jnp.floor(place * (1.0 / 128.0))
            low = place - 128.0 * high
            both = jnp.dot(
                jnp.concatenate([high.astype(bf16), low.astype(bf16)], axis=1), spread, preferred_element_type=f32
            )
            found = jnp.where(both[:, 128:] == lane_f, both[:, :128], -1.0)
            code[h * CHUNK + p * piece : h * CHUNK + (p + 1) * piece, :] = found.astype(bf16)


def order_kernel(got, ids, code, lhs, places, swap, raw):
    half = lhs.shape[0] // 2
    slots = lhs.shape[1]
    fill_swap(swap)
    batch = 8
    for first in range(0, slots // 128, batch):
        wide = jnp.concatenate(
            [
                jnp.concatenate([got[4 * (first + g) + i].astype(f32) for g in range(batch)], axis=0).astype(bf16)
                for i in range(4)
            ],
            axis=1,
        )
        moved = jnp.dot(wide, swap[...], preferred_element_type=f32)
        for g in range(batch):
            lanes = slice((first + g) * 128, (first + g) * 128 + 128)
            for q in range(4):
                count = 24 if q < 3 else 8
                raw[24 * q : 24 * q + count, lanes] = moved[24 * g : 24 * g + count, 128 * q : 128 * q + 128]
    cells = ids[...]
    raw[76:77, :] = (cells & 127).astype(f32)
    raw[77:78, :] = (cells >> 7).astype(f32)
    one, zero = jnp.ones((), bf16), jnp.zeros((), bf16)
    for h in range(slots // CHUNK):
        block = raw[:, h * CHUNK : (h + 1) * CHUNK].astype(bf16)
        part = code[h * CHUNK : (h + 1) * CHUNK, :]
        for p in range(CHUNK // 256):
            one_hot = jnp.concatenate(
                [jnp.where(part == jnp.asarray(2 * p + a, bf16), one, zero) for a in range(2)], axis=1
            )
            done = jnp.dot(block, one_hot, preferred_element_type=f32)
            lanes = slice(h * CHUNK + p * 256, h * CHUNK + (p + 1) * 256)
            places[:, lanes] = done[72:80, :]
            for t in range(4):
                hi, lo = split(done[:72] * done[72 + t : 73 + t, :])
                lhs[72 * t : 72 * t + 72, lanes] = hi
                lhs[half + 72 * t : half + 72 * t + 72, lanes] = lo


def forcing_kernel(starts, lhs, places, adjoint_hbm, state, x_low, x_high, adjoint, turned, arrived):
    copy = pltpu.make_async_copy(adjoint_hbm, adjoint, arrived)
    copy.start()
    fields = state.shape[0]
    chunks = lhs.shape[1] // CHUNK
    last = CHUNK // 128 - 2
    steps = state.shape[1] // 8
    row = lax.broadcasted_iota(jnp.int32, (128, 256), 0).astype(f32)
    window = lax.broadcasted_iota(jnp.int32, (1, 256), 1)

    def product(base, lon, skip):
        lat = places[4:5, pl.ds(base, 256)]
        slot_lon = places[5:6, pl.ds(base, 256)]
        if skip is not None:
            slot_lon = jnp.where(window >= skip, slot_lon, -1.0)
        one_hot = jnp.concatenate(
            [
                jnp.where(jnp.where(slot_lon == (lon + a).astype(f32), lat, -1.0) == row, 1.0, 0.0).astype(bf16)
                for a in range(2)
            ],
            axis=0,
        )
        both = lax.dot_general(
            lhs[:, pl.ds(base, 256)], one_hot, (((1,), (1,)), ((), ())), preferred_element_type=f32
        )
        return both

    def extent(h, number):
        low = starts[8 * h, number]
        high = starts[8 * h, number + 1]
        first = jnp.minimum(low >> 7, last)
        return first, jnp.maximum(((high + 127) >> 7) - first - 1, 0) >> 1

    def eight(step, _):
        rest = jnp.int32(0)
        for pair in range(4):
            number = step * 4 + pair
            total = None
            for h in range(chunks):
                first, visits = extent(h, number)
                rest = rest + visits
                piece = product(pl.multiple_of(h * CHUNK + first * 128, 128), 2 * number, None)
                total = piece if total is None else total + piece
            total = total[:fields] + total[fields:]
            for a in range(2):
                turned[pl.ds(2 * pair + a, fields, stride=9), :] = total[:, 128 * a : 128 * a + 128]

        @pl.when(rest > 0)
        def _():
            def each(n, _):
                pair, h = n // chunks, n % chunks
                number = step * 4 + pair
                first, visits = extent(h, number)

                def more(j, _):
                    at = first + 2 + 2 * j
                    start = jnp.minimum(at, last)
                    base = pl.multiple_of(h * CHUNK + start * 128, 128)
                    both = product(base, 2 * number, (at - start) * 128)
                    both = both[:fields] + both[fields:]
                    for a in range(2):
                        place = pl.ds(2 * pair + a, fields, stride=9)
                        turned[place, :] = turned[place, :] + both[:, 128 * a : 128 * a + 128]
                    return 0

                lax.fori_loop(0, visits, more, 0)
                return 0

            lax.fori_loop(0, 4 * chunks, each, 0)

        @pl.when(step == 0)
        def _():
            copy.wait()

        rows = pl.ds(pl.multiple_of(8 * step, 8), 8)
        for f in range(fields):
            cell = adjoint[f, rows, :] + turned[9 * f : 9 * f + 8, :]
            state[f, rows, :] = cell
            turned[9 * f : 9 * f + 8, :] = cell

        def edge(out, order):
            near, second, third = (turned[pl.ds(j, fields, stride=9), :] for j in order)
            out[0], out[1] = split(near)
            out[2] = second.astype(bf16)
            out[3] = third.astype(bf16)

        @pl.when(step == 0)
        def _():
            edge(x_low, (0, 1, 2))

        @pl.when(step == steps - 1)
        def _():
            edge(x_high, (7, 6, 5))

        return 0

    lax.fori_loop(0, steps, eight, 0)


def zonal_rows(outer, state, courant, spread, halos, zonal, to_left, to_right, halves, pad):
    lane = lax.broadcasted_iota(jnp.int32, (16, 128), 1)
    group = lane >> 2
    note_rows = slice(16, 32) if outer else slice(0, 16)

    def block(b, _):
        levels = pl.ds(pl.multiple_of(b * LB, LB), LB)
        if outer:
            for t in range(4):
                for side, halo in enumerate(halos):
                    near = halo[0, t, levels, :].astype(f32) + halo[1, t, levels, :].astype(f32)
                    far = (halo[2, t, levels, :].astype(f32), halo[3, t, levels, :].astype(f32))
                    for k, value in enumerate((near, *far)):
                        pad[pl.ds(t * LB * 33 + (24 + k if side else 7 - k), LB, stride=33), :] = value
        notes = [jnp.zeros((16, 128), f32)] * 2
        for t in range(4):
            for l in range(LB):
                level = b * LB + l
                i = t * LB + l
                if outer:
                    c = jnp.concatenate([courant[level, 0:8, :], courant[level, 24:32, :]], axis=0)
                    low = state[t, level, 0:8, :]
                    high = state[t, level, 24:32, :]
                    base = 33 * i
                    pad[base + 8 : base + 16, :] = low
                    pad[base + 16 : base + 24, :] = high
                    v = {0: jnp.concatenate([low, high], axis=0)}
                    for k in (1, 2, 3):
                        v[-k] = jnp.concatenate(
                            [pad[base + 8 - k : base + 16 - k, :], state[t, level, 24 - k : 32 - k, :]], axis=0
                        )
                        v[k] = jnp.concatenate(
                            [state[t, level, k : 8 + k, :], pad[base + 16 + k : base + 24 + k, :]], axis=0
                        )
                else:
                    c = courant[level, 8:24, :]
                    v = {k: state[t, level, 8 + k : 24 + k, :] for k in range(-3, 4)}
                out = stencil(v, c, 0.5 * c * c)
                if outer:
                    zonal[t, level, 0:8, :] = out[:8]
                    zonal[t, level, 24:32, :] = out[8:]
                else:
                    zonal[t, level, 8:24, :] = out
                at = slice(16 * i, 16 * i + 16)
                halves[at, 0:128], halves[at, 128:256] = split(out)
            at = slice(16 * LB * t, 16 * LB * (t + 1))
            edges = jnp.dot(halves[at, :], spread[...], preferred_element_type=f32)
            for l in range(LB):
                mine = group == t * LB + l
                rows = slice(16 * l, 16 * l + 16)
                notes = [jnp.where(mine, edges[rows, 128 * n : 128 * n + 128], notes[n]) for n in range(2)]
        to_left[b, note_rows] = notes[0].astype(bf16)
        to_right[b, note_rows] = notes[1].astype(bf16)
        return 0

    lax.fori_loop(0, courant.shape[0] // LB, block, 0)


def inner_kernel(state, courant, spread, zonal, to_left, to_right, halves):
    zonal_rows(False, state, courant, spread, None, zonal, to_left, to_right, halves, None)


def outer_kernel(state, courant, spread, left, right, _z, _l, _r, zonal, to_left, to_right, halves, pad):
    zonal_rows(True, state, courant, spread, (left, right), zonal, to_left, to_right, halves, pad)


def stencil(v, c, c2):
    slope = D1 * (v[1] - v[-1]) + D2 * (v[2] - v[-2]) + D3 * (v[3] - v[-3])
    curve = E0 * v[0] + E1 * (v[1] + v[-1]) + E2 * (v[2] + v[-2]) + E3 * (v[3] + v[-3])
    return v[0] + c * slope + c2 * curve


def lat_kernel(zonal, courant, weights, result, halves):
    tracers, levels, lons, lats = zonal.shape
    rows = tracers * lons

    def block(b, _):
        for l in range(LB):
            level = b * LB + l
            at = slice(l * rows, (l + 1) * rows)
            halves[at, 0:128], halves[at, 128:256] = split(zonal[:, level].reshape(rows, lats))
        for l in range(LB):
            level = b * LB + l
            at = slice(l * rows, (l + 1) * rows)
            both = jnp.dot(halves[at, :], weights[...], preferred_element_type=f32).reshape(tracers, lons, 256)
            c = courant[level]
            result[:, level] = (
                zonal[:, level] + (c * (1.0 / 60.0)) * both[:, :, :128] + (c * c * (1.0 / 360.0)) * both[:, :, 128:]
            )
        return 0

    lax.fori_loop(0, levels // LB, block, 0)


def column_kernel(first, inner, courant, mixing, inv, q, left, right, weights, *rest):
    lhs = rest[-1]
    if first:
        state, gradient, x_low, x_high = rest[:-1]
    else:
        before, state, gradient = rest[:-1]
    levels = inv.shape[0]
    rows = 32
    lane = lax.broadcasted_iota(jnp.int32, (rows, 128), 1)
    row = lax.broadcasted_iota(jnp.int32, (rows, 128), 0)
    owner = ((lane >> 2) - (row >> 3) * LB).astype(f32).astype(bf16)
    zero = jnp.zeros((), bf16)

    def tile(r, _):
        here = pl.ds(pl.multiple_of(8 * r, 8), 8)
        slot = jnp.where(r == 0, 2, jnp.where(r == 3, 3, r - 1))
        there = pl.ds(pl.multiple_of(8 * slot, 8), 8)
        carry = None
        for b in range(levels // LB):
            notes = [
                jnp.concatenate([side[b, there, :].astype(f32)] * 4, axis=0).astype(bf16) for side in (left, right)
            ]
            for l in range(LB):
                at = slice((b * LB + l) * rows, (b * LB + l + 1) * rows)
                mine = owner == jnp.asarray(l, bf16)
                lhs[at, 0:128] = jnp.where(mine, notes[0], zero)
                lhs[at, 128:256] = jnp.where(mine, notes[1], zero)
            both = jnp.dot(
                lhs[b * LB * rows : (b + 1) * LB * rows, :], weights[...], preferred_element_type=f32
            )
            for l in range(LB):
                level = b * LB + l
                c = courant[level, here, :]
                part = both[l * rows : l * rows + rows].reshape(4, 8, 256)
                y = inner[:, level, here, :]
                y = y + (c * (1.0 / 60.0)) * part[:, :, :128] + (c * c * (1.0 / 360.0)) * part[:, :, 128:]
                if level > 0:
                    y = y + mixing[level - 1, here, :] * carry
                carry = y * inv[level, here, :]
                state[:, level, here, :] = carry

        def back(j, carry):
            level = levels - 2 - j
            carry = state[:, level, here, :] + q[level, here, :] * carry
            state[:, level, here, :] = carry
            return carry

        carry = lax.fori_loop(0, levels - 1, back, carry, unroll=8)
        gradient[:, here, :] = carry if first else before[:, here, :] + carry
        return 0

    lax.fori_loop(0, inner.shape[2] // 8, tile, 0)
    if first:
        for out, order in ((x_low, (0, 1, 2)), (x_high, (31, 30, 29))):
            for t in range(4):
                rows = slice(levels * t, levels * t + levels)
                near, second, third = (state[t, :, j, :] for j in order)
                out[0, rows], out[1, rows] = split(near)
                out[2, rows] = second.astype(bf16)
                out[3, rows] = third.astype(bf16)


def edge_weights():
    table = np.zeros((256, 256), np.float32)
    for lane in range(128):
        part = lane % 4
        table[(128, part)[part < 3], lane] = 1
        table[(255, 125 + part)[part < 3], 128 + lane] = 1
    return table


def lat_weights():
    first = {1: 45, 2: -9, 3: 1}
    second = {0: -490, 1: 270, 2: -27, 3: 2}
    table = np.zeros((512, 256), np.float32)

    def fill(row, place):
        for out in range(128):
            k = place - out
            if abs(k) <= 3:
                table[row, out] = first.get(abs(k), 0) * (1 if k > 0 else -1)
                table[row, 128 + out] = second[abs(k)]

    for lane in range(128):
        fill(lane, lane)
        fill(128 + lane, lane)
        fill(256 + lane, (-3, -2, -1, -1)[lane % 4])
        fill(384 + lane, (128, 129, 130, 128)[lane % 4])
    return table


def cost(flops, size):
    return pl.CostEstimate(flops=flops, bytes_accessed=size, transcendentals=0)


def params(mib):
    return pltpu.CompilerParams(vmem_limit_bytes=mib * 2**20)


def shape(dims, kind=f32):
    return jax.ShapeDtypeStruct(dims, kind)


def shift(value, axis, closed, forward):
    count = lax.axis_size(axis)
    ends = count if closed else count - 1
    pairs = [(i, (i + 1) % count) for i in range(ends)]
    if not forward:
        pairs = [(b, a) for a, b in pairs]
    return lax.ppermute(value, axis, pairs)


def local(adjoint_in, courant_x, courant_y, mixing, kernel_rows, tracer_weights, column_ids, counts):
    tracers, levels, lons, lats = adjoint_in.shape
    devices = lax.axis_size(("gx", "gy"))
    slots = kernel_rows.shape[1]
    fields = tracers * levels
    size = fields * lons * lats * 4

    packed = pl.pallas_call(
        pack_kernel,
        grid=(2,),
        in_specs=[
            pl.BlockSpec(memory_space=pltpu.SMEM),
            pl.BlockSpec((levels, slots // 2), lambda i: (0, i)),
            pl.BlockSpec((tracers, slots // 2), lambda i: (0, i)),
        ],
        out_specs=pl.BlockSpec((devices // 2, 24, 128), lambda i: (i, 0, 0)),
        out_shape=shape((devices, 24, 128), bf16),
        scratch_shapes=[pltpu.VMEM((512, 512), bf16)],
        compiler_params=params(60),
        name="pack",
    )(counts, kernel_rows, tracer_weights)
    got = lax.all_to_all(packed, ("gx", "gy"), split_axis=0, concat_axis=0, tiled=True)

    inv, q = pl.pallas_call(
        factor_kernel,
        out_shape=[shape((levels, lons, lats))] * 2,
        compiler_params=params(16),
        cost_estimate=cost(30 * levels * lons * lats, 3 * levels * lons * lats * 4),
        name="factor",
    )(mixing)
    bins = jnp.broadcast_to((column_ids // (2 * lats)).astype(bf16)[:, None], (slots, 128))
    code, starts = pl.pallas_call(
        rank_kernel,
        out_shape=[shape((slots, 128), bf16), shape((8 * (slots // CHUNK), 128), jnp.int32)],
        compiler_params=params(16),
        cost_estimate=cost(10**9, 2 * 10**6),
        name="rank",
    )(bins)
    lhs, places = pl.pallas_call(
        order_kernel,
        out_shape=[shape((2 * fields, slots), bf16), shape((8, slots))],
        scratch_shapes=[pltpu.VMEM((512, 512), bf16), pltpu.VMEM((80, slots), f32)],
        compiler_params=params(24),
        cost_estimate=cost(10**9, 8 * 10**6),
        name="order",
    )(got, column_ids.reshape(1, slots), code)

    vmem = pl.BlockSpec(memory_space=pltpu.VMEM)
    edge = shape((4, fields, lats), bf16)
    state, x_low, x_high = pl.pallas_call(
        forcing_kernel,
        in_specs=[pl.BlockSpec(memory_space=pltpu.SMEM), vmem, vmem, pl.BlockSpec(memory_space=pl.ANY)],
        out_specs=[vmem] * 3,
        out_shape=[shape((fields, lons, lats)), edge, edge],
        scratch_shapes=[
            pltpu.VMEM((fields, lons, lats), f32),
            pltpu.VMEM((fields * 9, lats), f32),
            pltpu.SemaphoreType.DMA,
        ],
        compiler_params=params(40),
        cost_estimate=cost(10**10, 2 * size),
        name="forcing",
    )(starts, lhs, places, adjoint_in.reshape(fields, lons, lats))

    whole_field = shape((tracers, levels, lons, lats))
    blocks = levels // LB
    note = shape((blocks, lons, 128), bf16)
    spread = jnp.asarray(edge_weights(), bf16)
    table = lat_weights()
    for step in range(STEPS):
        from_left = shift(x_high, "gx", True, True)
        from_right = shift(x_low, "gx", True, False)
        halves = pltpu.VMEM((tracers * LB * 16, 2 * lats), bf16)
        state = state.reshape(tracers, levels, lons, lats)
        partial = pl.pallas_call(
            inner_kernel,
            in_specs=[vmem] * 3,
            out_specs=[vmem] * 3,
            out_shape=[whole_field, note, note],
            scratch_shapes=[halves],
            compiler_params=params(24),
            cost_estimate=cost(5 * size, 2 * size),
            name="inner",
        )(state, courant_x, spread)
        zonal, to_left, to_right = pl.pallas_call(
            outer_kernel,
            in_specs=[vmem] * 8,
            out_specs=[vmem] * 3,
            out_shape=[whole_field, note, note],
            input_output_aliases={5: 0, 6: 1, 7: 2},
            scratch_shapes=[halves, pltpu.VMEM((tracers * LB * 33, lats), f32)],
            compiler_params=params(24),
            cost_estimate=cost(5 * size, 2 * size),
            name="outer",
        )(
            state,
            courant_x,
            spread,
            from_left.reshape(4, tracers, levels, lats),
            from_right.reshape(4, tracers, levels, lats),
            *partial,
        )
        y_left = shift(to_right, "gy", False, True)
        y_right = shift(to_left, "gy", False, False)
        inner = pl.pallas_call(
            lat_kernel,
            in_specs=[vmem] * 3,
            out_specs=vmem,
            out_shape=whole_field,
            scratch_shapes=[pltpu.VMEM((LB * tracers * lons, 2 * lats), bf16)],
            compiler_params=params(24),
            cost_estimate=cost(5 * size, 2 * size),
            name="lat",
        )(zonal, courant_y, jnp.asarray(table[:256], bf16))
        first = step == 0
        operands = [inner, courant_y, mixing, inv, q, y_left, y_right, jnp.asarray(table[256:], bf16)]
        out_shape = [whole_field, shape((tracers, lons, lats))]
        if first:
            out_shape += [edge, edge]
        else:
            operands.append(gradient)

        def kernel(*refs, first=first):
            column_kernel(first, *refs)

        out = pl.pallas_call(
            kernel,
            in_specs=[vmem] * len(operands),
            out_specs=[vmem] * len(out_shape),
            out_shape=out_shape,
            scratch_shapes=[pltpu.VMEM((levels * tracers * 8, 2 * lats), bf16)],
            compiler_params=params(24),
            cost_estimate=cost(5 * size, 2 * size),
            name="column",
        )(*operands)
        if first:
            state, gradient, x_low, x_high = out
        else:
            state, gradient = out
    return state, gradient


def solution(mesh):
    in_specs = (
        P(None, None, "gx", "gy"),
        P(None, "gx", "gy"),
        P(None, "gx", "gy"),
        P(None, "gx", "gy"),
        P(None, ("gx", "gy")),
        P(None, ("gx", "gy")),
        P(("gx", "gy")),
        P(("gx", "gy"), None),
    )
    out_specs = (P(None, None, "gx", "gy"), P(None, "gx", "gy"))
    return jax.shard_map(local, mesh=mesh, in_specs=in_specs, out_specs=out_specs, check_vma=False)
```

```python
import jax
import jax.numpy as jnp
import numpy as np
from jax import lax
from jax.experimental import pallas as pl
from jax.experimental.pallas import tpu as pltpu
from jax.sharding import PartitionSpec as P

STEPS = 2
LB = 8
CHUNK = 1024

D1, D2, D3 = 0.75, -0.15, 1.0 / 60.0
E1, E2, E3 = 1.5, -0.15, 1.0 / 90.0
E0 = -49.0 / 18.0

f32 = jnp.float32
bf16 = jnp.bfloat16


def fill_swap(table):
    row = lax.broadcasted_iota(jnp.int32, table.shape, 0)
    col = lax.broadcasted_iota(jnp.int32, table.shape, 1)
    want = ((col >> 5) & 3) * 128 + (col >> 7) * 32 + (col & 31)
    table[...] = jnp.where(row == want, 1.0, 0.0).astype(bf16)


def is_odd(axis):
    return (lax.axis_index(axis) & 1) == 1


def split(value):
    hi = value.astype(bf16)
    return hi, (value - hi.astype(f32)).astype(bf16)


def pack_kernel(counts, rows, weights, out, swap):
    step = pl.program_id(0)
    groups = rows.shape[1] // 128

    @pl.when(step == 0)
    def _():
        fill_swap(swap)

    lane = lax.broadcasted_iota(jnp.int32, (24, 128), 1)
    block = lane >> 5
    columns = [[] for _ in range(4)]
    for g in range(groups):
        lanes = slice(g * 128, g * 128 + 128)
        first = 4 * (step * groups + g)
        limit = jnp.where(
            block < 2,
            jnp.where(block == 0, counts[0, first], counts[0, first + 1]),
            jnp.where(block == 2, counts[0, first + 2], counts[0, first + 3]),
        )
        live = (lane & 31) < limit
        for q in range(3):
            columns[q].append(jnp.where(live, rows[24 * q : 24 * q + 24, lanes].astype(f32), 0.0))
        columns[3].append(jnp.concatenate([weights[:, lanes].astype(f32), jnp.zeros((20, 128), f32)], axis=0))
    wide = jnp.concatenate([jnp.concatenate(c, axis=0).astype(bf16) for c in columns], axis=1)
    moved = jnp.dot(wide, swap[...], preferred_element_type=f32)
    for g in range(groups):
        for i in range(4):
            out[4 * g + i] = moved[24 * g : 24 * g + 24, 128 * i : 128 * i + 128].astype(bf16)


def factor_kernel(mixing, inv_out, q_out):
    levels = inv_out.shape[0]
    top = mixing[0]
    inv = 1.0 / (1.0 + top)
    q = top * inv
    inv_out[0] = inv
    q_out[0] = q

    def level(l, carry):
        below, q = carry
        above = mixing[l]
        inv = 1.0 / (1.0 + below + above - below * q)
        q = above * inv
        inv_out[l] = inv
        q_out[l] = q
        return above, q

    below, q = lax.fori_loop(1, levels - 1, level, (top, q))
    inv_out[levels - 1] = 1.0 / (1.0 + below - below * q)
    q_out[levels - 1] = jnp.zeros_like(q)


def rank_kernel(bins, code, starts):
    piece = 256
    lane = lax.broadcasted_iota(jnp.int32, (piece, 128), 1)
    lane_f = lane.astype(f32)
    upto = (lax.broadcasted_iota(jnp.int32, (piece, piece), 1) <= lax.broadcasted_iota(jnp.int32, (piece, piece), 0))
    upto = jnp.where(upto, 1.0, 0.0).astype(bf16)
    row2 = lax.broadcasted_iota(jnp.int32, (256, 256), 0)
    col2 = lax.broadcasted_iota(jnp.int32, (256, 256), 1)
    spread = jnp.where((row2 >> 7) == (col2 >> 7), 1.0, 0.0).astype(bf16)
    ones = jnp.ones((8, CHUNK), bf16)
    for h in range(bins.shape[0] // CHUNK):
        own = bins[h * CHUNK : (h + 1) * CHUNK, :].astype(f32)
        wide = lax.broadcasted_iota(jnp.int32, own.shape, 1).astype(f32)
        below = jnp.where(own < wide, 1.0, 0.0).astype(bf16)
        start = jnp.dot(ones, below, preferred_element_type=f32)
        starts[8 * h : 8 * h + 8, :] = start.astype(jnp.int32)
        running = start[0:1, :] - 1.0
        for p in range(CHUNK // piece):
            at = slice(p * piece, p * piece + piece)
            mine = own[at] == lane_f
            one_hot = jnp.where(mine, 1.0, 0.0)
            place = jnp.dot(upto, one_hot.astype(bf16), preferred_element_type=f32) + running
            running = place[piece - 1 : piece, :]
            place = jnp.where(mine, place, 0.0)
            high = jnp.floor(place * (1.0 / 128.0))
            low = place - 128.0 * high
            both = jnp.dot(
                jnp.concatenate([high.astype(bf16), low.astype(bf16)], axis=1), spread, preferred_element_type=f32
            )
            found = jnp.where(both[:, 128:] == lane_f, both[:, :128], -1.0)
            code[h * CHUNK + p * piece : h * CHUNK + (p + 1) * piece, :] = found.astype(bf16)


def order_kernel(got, ids, code, lhs, places, swap, raw):
    half = lhs.shape[0] // 2
    slots = lhs.shape[1]
    fill_swap(swap)
    batch = 8
    for first in range(0, slots // 128, batch):
        wide = jnp.concatenate(
            [
                jnp.concatenate([got[4 * (first + g) + i].astype(f32) for g in range(batch)], axis=0).astype(bf16)
                for i in range(4)
            ],
            axis=1,
        )
        moved = jnp.dot(wide, swap[...], preferred_element_type=f32)
        for g in range(batch):
            lanes = slice((first + g) * 128, (first + g) * 128 + 128)
            for q in range(4):
                count = 24 if q < 3 else 8
                raw[24 * q : 24 * q + count, lanes] = moved[24 * g : 24 * g + count, 128 * q : 128 * q + 128]
    cells = ids[...]
    raw[76:77, :] = (cells & 127).astype(f32)
    raw[77:78, :] = (cells >> 7).astype(f32)
    one, zero = jnp.ones((), bf16), jnp.zeros((), bf16)
    for h in range(slots // CHUNK):
        block = raw[:, h * CHUNK : (h + 1) * CHUNK].astype(bf16)
        part = code[h * CHUNK : (h + 1) * CHUNK, :]
        for p in range(CHUNK // 256):
            one_hot = jnp.concatenate(
                [jnp.where(part == jnp.asarray(2 * p + a, bf16), one, zero) for a in range(2)], axis=1
            )
            done = jnp.dot(block, one_hot, preferred_element_type=f32)
            lanes = slice(h * CHUNK + p * 256, h * CHUNK + (p + 1) * 256)
            places[:, lanes] = done[72:80, :]
            for t in range(4):
                hi, lo = split(done[:72] * done[72 + t : 73 + t, :])
                lhs[72 * t : 72 * t + 72, lanes] = hi
                lhs[half + 72 * t : half + 72 * t + 72, lanes] = lo


def forcing_kernel(starts, lhs, places, adjoint_hbm, state, x_a, x_b, adjoint, turned, arrived):
    copy = pltpu.make_async_copy(adjoint_hbm, adjoint, arrived)
    copy.start()
    fields = state.shape[0]
    chunks = lhs.shape[1] // CHUNK
    last = CHUNK // 128 - 2
    steps = state.shape[1] // 8
    row = lax.broadcasted_iota(jnp.int32, (128, 256), 0).astype(f32)
    window = lax.broadcasted_iota(jnp.int32, (1, 256), 1)

    def placed(base, lon, skip):
        lat = places[4:5, pl.ds(base, 256)]
        slot_lon = places[5:6, pl.ds(base, 256)]
        if skip is not None:
            slot_lon = jnp.where(window >= skip, slot_lon, -1.0)
        return jnp.concatenate(
            [
                jnp.where(jnp.where(slot_lon == (lon + a).astype(f32), lat, -1.0) == row, 1.0, 0.0).astype(bf16)
                for a in range(2)
            ],
            axis=0,
        )

    def product(bases, one_hots):
        values = [lhs[at, pl.ds(base, 256)] for at in (slice(0, fields), slice(fields, 2 * fields)) for base in bases]
        return lax.dot_general(
            jnp.concatenate(values, axis=1),
            jnp.concatenate(one_hots * 2, axis=1),
            (((1,), (1,)), ((), ())),
            preferred_element_type=f32,
        )

    def extent(h, number):
        low = starts[8 * h, number]
        high = starts[8 * h, number + 1]
        first = jnp.minimum(low >> 7, last)
        return first, jnp.maximum(((high + 127) >> 7) - first - 1, 0) >> 1

    def eight(step, _):
        rest = jnp.int32(0)
        for pair in range(4):
            number = step * 4 + pair
            bases = []
            for h in range(chunks):
                first, visits = extent(h, number)
                rest = rest + visits
                bases.append(pl.multiple_of(h * CHUNK + first * 128, 128))
            total = product(bases, [placed(base, 2 * number, None) for base in bases])
            for a in range(2):
                turned[pl.ds(2 * pair + a, fields, stride=9), :] = total[:, 128 * a : 128 * a + 128]

        @pl.when(rest > 0)
        def _():
            def each(n, _):
                pair, h = n // chunks, n % chunks
                number = step * 4 + pair
                first, visits = extent(h, number)

                def more(j, _):
                    at = first + 2 + 2 * j
                    start = jnp.minimum(at, last)
                    base = pl.multiple_of(h * CHUNK + start * 128, 128)
                    both = product([base], [placed(base, 2 * number, (at - start) * 128)])
                    for a in range(2):
                        place = pl.ds(2 * pair + a, fields, stride=9)
                        turned[place, :] = turned[place, :] + both[:, 128 * a : 128 * a + 128]
                    return 0

                lax.fori_loop(0, visits, more, 0)
                return 0

            lax.fori_loop(0, 4 * chunks, each, 0)

        @pl.when(step == 0)
        def _():
            copy.wait()

        rows = pl.ds(pl.multiple_of(8 * step, 8), 8)
        for f in range(fields):
            cell = adjoint[f, rows, :] + turned[9 * f : 9 * f + 8, :]
            state[f, rows, :] = cell
            turned[9 * f : 9 * f + 8, :] = cell

        def edge(out, order):
            near, second, third = (turned[pl.ds(j, fields, stride=9), :] for j in order)
            out[0], out[1] = split(near)
            out[2] = second.astype(bf16)
            out[3] = third.astype(bf16)

        odd = is_odd("gx")
        for when, order, swapped in ((0, (0, 1, 2), odd), (steps - 1, (7, 6, 5), jnp.logical_not(odd))):
            for out, mine in ((x_a, swapped), (x_b, jnp.logical_not(swapped))):

                @pl.when((step == when) & mine)
                def _(out=out, order=order):
                    edge(out, order)

        return 0

    lax.fori_loop(0, steps, eight, 0)


def zonal_rows(outer, state, courant, spread, halos, zonal, to_a, to_b, halves, pad):
    lane = lax.broadcasted_iota(jnp.int32, (16, 128), 1)
    group = lane >> 2
    note_rows = slice(16, 32) if outer else slice(0, 16)
    odd_x = is_odd("gx")
    odd_y = is_odd("gy")

    def block(b, _):
        levels = pl.ds(pl.multiple_of(b * LB, LB), LB)
        if outer:
            for t in range(4):
                parts = []
                for halo in halos:
                    part = [halo[n, t, levels, :].astype(f32) for n in range(4)]
                    parts.append((part[0] + part[1], part[2], part[3]))
                for side in range(2):
                    for k in range(3):
                        value = jnp.where(odd_x, parts[side][k], parts[1 - side][k])
                        pad[pl.ds(t * LB * 33 + (24 + k if side else 7 - k), LB, stride=33), :] = value
        notes = [jnp.zeros((16, 128), f32)] * 2
        for t in range(4):
            for l in range(LB):
                level = b * LB + l
                i = t * LB + l
                if outer:
                    c = jnp.concatenate([courant[level, 0:8, :], courant[level, 24:32, :]], axis=0)
                    low = state[t, level, 0:8, :]
                    high = state[t, level, 24:32, :]
                    base = 33 * i
                    pad[base + 8 : base + 16, :] = low
                    pad[base + 16 : base + 24, :] = high
                    v = {0: jnp.concatenate([low, high], axis=0)}
                    for k in (1, 2, 3):
                        v[-k] = jnp.concatenate(
                            [pad[base + 8 - k : base + 16 - k, :], state[t, level, 24 - k : 32 - k, :]], axis=0
                        )
                        v[k] = jnp.concatenate(
                            [state[t, level, k : 8 + k, :], pad[base + 16 + k : base + 24 + k, :]], axis=0
                        )
                else:
                    c = courant[level, 8:24, :]
                    v = {k: state[t, level, 8 + k : 24 + k, :] for k in range(-3, 4)}
                out = stencil(v, c, 0.5 * c * c)
                if outer:
                    zonal[t, level, 0:8, :] = out[:8]
                    zonal[t, level, 24:32, :] = out[8:]
                else:
                    zonal[t, level, 8:24, :] = out
                at = slice(16 * i, 16 * i + 16)
                halves[at, 0:128], halves[at, 128:256] = split(out)
            at = slice(16 * LB * t, 16 * LB * (t + 1))
            edges = jnp.dot(halves[at, :], spread[...], preferred_element_type=f32)
            for l in range(LB):
                mine = group == t * LB + l
                rows = slice(16 * l, 16 * l + 16)
                notes = [jnp.where(mine, edges[rows, 128 * n : 128 * n + 128], notes[n]) for n in range(2)]
        to_a[b, note_rows] = jnp.where(odd_y, notes[0], notes[1]).astype(bf16)
        to_b[b, note_rows] = jnp.where(odd_y, notes[1], notes[0]).astype(bf16)
        return 0

    lax.fori_loop(0, courant.shape[0] // LB, block, 0)


def inner_kernel(state, courant, spread, zonal, to_a, to_b, halves):
    zonal_rows(False, state, courant, spread, None, zonal, to_a, to_b, halves, None)


def outer_kernel(state, courant, spread, from_a, from_b, _z, _a, _b, zonal, to_a, to_b, halves, pad):
    zonal_rows(True, state, courant, spread, (from_a, from_b), zonal, to_a, to_b, halves, pad)


def stencil(v, c, c2):
    slope = D1 * (v[1] - v[-1]) + D2 * (v[2] - v[-2]) + D3 * (v[3] - v[-3])
    curve = E0 * v[0] + E1 * (v[1] + v[-1]) + E2 * (v[2] + v[-2]) + E3 * (v[3] + v[-3])
    return v[0] + c * slope + c2 * curve


def lat_kernel(zonal, courant, weights, result, halves):
    tracers, levels, lons, lats = zonal.shape
    rows = tracers * lons

    def block(b, _):
        for l in range(LB):
            level = b * LB + l
            at = slice(l * rows, (l + 1) * rows)
            halves[at, 0:128], halves[at, 128:256] = split(zonal[:, level].reshape(rows, lats))
        for l in range(LB):
            level = b * LB + l
            at = slice(l * rows, (l + 1) * rows)
            both = jnp.dot(halves[at, :], weights[...], preferred_element_type=f32).reshape(tracers, lons, 256)
            c = courant[level]
            result[:, level] = (
                zonal[:, level] + (c * (1.0 / 60.0)) * both[:, :, :128] + (c * c * (1.0 / 360.0)) * both[:, :, 128:]
            )
        return 0

    lax.fori_loop(0, levels // LB, block, 0)


def column_kernel(first, inner, courant, mixing, inv, q, from_a, from_b, weights, *rest):
    lhs = rest[-1]
    if first:
        state, gradient, x_a, x_b = rest[:-1]
    else:
        before, state, gradient = rest[:-1]
    levels = inv.shape[0]
    rows = 32
    lane = lax.broadcasted_iota(jnp.int32, (rows, 128), 1)
    row = lax.broadcasted_iota(jnp.int32, (rows, 128), 0)
    owner = ((lane >> 2) - (row >> 3) * LB).astype(f32).astype(bf16)
    zero = jnp.zeros((), bf16)
    odd_y = is_odd("gy")

    def tile(r, _):
        here = pl.ds(pl.multiple_of(8 * r, 8), 8)
        slot = jnp.where(r == 0, 2, jnp.where(r == 3, 3, r - 1))
        there = pl.ds(pl.multiple_of(8 * slot, 8), 8)
        carry = None
        for b in range(levels // LB):
            a, z = from_a[b, there, :].astype(f32), from_b[b, there, :].astype(f32)
            notes = [
                jnp.concatenate([note] * 4, axis=0).astype(bf16)
                for note in (jnp.where(odd_y, a, z), jnp.where(odd_y, z, a))
            ]
            for l in range(LB):
                at = slice((b * LB + l) * rows, (b * LB + l + 1) * rows)
                mine = owner == jnp.asarray(l, bf16)
                lhs[at, 0:128] = jnp.where(mine, notes[0], zero)
                lhs[at, 128:256] = jnp.where(mine, notes[1], zero)
            both = jnp.dot(
                lhs[b * LB * rows : (b + 1) * LB * rows, :], weights[...], preferred_element_type=f32
            )
            for l in range(LB):
                level = b * LB + l
                c = courant[level, here, :]
                part = both[l * rows : l * rows + rows].reshape(4, 8, 256)
                y = inner[:, level, here, :]
                y = y + (c * (1.0 / 60.0)) * part[:, :, :128] + (c * c * (1.0 / 360.0)) * part[:, :, 128:]
                if level > 0:
                    y = y + mixing[level - 1, here, :] * carry
                carry = y * inv[level, here, :]
                state[:, level, here, :] = carry

        def back(j, carry):
            level = levels - 2 - j
            carry = state[:, level, here, :] + q[level, here, :] * carry
            state[:, level, here, :] = carry
            return carry

        carry = lax.fori_loop(0, levels - 1, back, carry, unroll=8)
        gradient[:, here, :] = carry if first else before[:, here, :] + carry
        return 0

    lax.fori_loop(0, inner.shape[2] // 8, tile, 0)
    if first:

        def edge(out, order):
            for t in range(4):
                rows = slice(levels * t, levels * t + levels)
                near, second, third = (state[t, :, j, :] for j in order)
                out[0, rows], out[1, rows] = split(near)
                out[2, rows] = second.astype(bf16)
                out[3, rows] = third.astype(bf16)

        low, high = (0, 1, 2), (31, 30, 29)

        @pl.when(is_odd("gx"))
        def _():
            edge(x_a, low)
            edge(x_b, high)

        @pl.when(jnp.logical_not(is_odd("gx")))
        def _():
            edge(x_a, high)
            edge(x_b, low)


def edge_weights():
    table = np.zeros((256, 256), np.float32)
    for lane in range(128):
        part = lane % 4
        table[(128, part)[part < 3], lane] = 1
        table[(255, 125 + part)[part < 3], 128 + lane] = 1
    return table


def lat_weights():
    first = {1: 45, 2: -9, 3: 1}
    second = {0: -490, 1: 270, 2: -27, 3: 2}
    table = np.zeros((512, 256), np.float32)

    def fill(row, place):
        for out in range(128):
            k = place - out
            if abs(k) <= 3:
                table[row, out] = first.get(abs(k), 0) * (1 if k > 0 else -1)
                table[row, 128 + out] = second[abs(k)]

    for lane in range(128):
        fill(lane, lane)
        fill(128 + lane, lane)
        fill(256 + lane, (-3, -2, -1, -1)[lane % 4])
        fill(384 + lane, (128, 129, 130, 128)[lane % 4])
    return table


def cost(flops, size):
    return pl.CostEstimate(flops=flops, bytes_accessed=size, transcendentals=0)


def params(mib):
    return pltpu.CompilerParams(vmem_limit_bytes=mib * 2**20)


def shape(dims, kind=f32):
    return jax.ShapeDtypeStruct(dims, kind)


def swap(value, axis, first, closed):
    count = lax.axis_size(axis)
    pairs = []
    for low in range(0 if first else 1, count, 2):
        if low + 1 < count or closed:
            high = (low + 1) % count
            pairs += [(low, high), (high, low)]
    return lax.ppermute(value, axis, pairs)


def local(adjoint_in, courant_x, courant_y, mixing, kernel_rows, tracer_weights, column_ids, counts):
    tracers, levels, lons, lats = adjoint_in.shape
    devices = lax.axis_size(("gx", "gy"))
    slots = kernel_rows.shape[1]
    fields = tracers * levels
    size = fields * lons * lats * 4

    packed = pl.pallas_call(
        pack_kernel,
        grid=(2,),
        in_specs=[
            pl.BlockSpec(memory_space=pltpu.SMEM),
            pl.BlockSpec((levels, slots // 2), lambda i: (0, i)),
            pl.BlockSpec((tracers, slots // 2), lambda i: (0, i)),
        ],
        out_specs=pl.BlockSpec((devices // 2, 24, 128), lambda i: (i, 0, 0)),
        out_shape=shape((devices, 24, 128), bf16),
        scratch_shapes=[pltpu.VMEM((512, 512), bf16)],
        compiler_params=params(60),
        name="pack",
    )(counts, kernel_rows, tracer_weights)
    got = lax.all_to_all(packed, ("gx", "gy"), split_axis=0, concat_axis=0, tiled=True)

    inv, q = pl.pallas_call(
        factor_kernel,
        out_shape=[shape((levels, lons, lats))] * 2,
        compiler_params=params(16),
        cost_estimate=cost(30 * levels * lons * lats, 3 * levels * lons * lats * 4),
        name="factor",
    )(mixing)
    bins = jnp.broadcast_to((column_ids // (2 * lats)).astype(bf16)[:, None], (slots, 128))
    code, starts = pl.pallas_call(
        rank_kernel,
        out_shape=[shape((slots, 128), bf16), shape((8 * (slots // CHUNK), 128), jnp.int32)],
        compiler_params=params(16),
        cost_estimate=cost(10**9, 2 * 10**6),
        name="rank",
    )(bins)
    lhs, places = pl.pallas_call(
        order_kernel,
        out_shape=[shape((2 * fields, slots), bf16), shape((8, slots))],
        scratch_shapes=[pltpu.VMEM((512, 512), bf16), pltpu.VMEM((80, slots), f32)],
        compiler_params=params(24),
        cost_estimate=cost(10**9, 8 * 10**6),
        name="order",
    )(got, column_ids.reshape(1, slots), code)

    vmem = pl.BlockSpec(memory_space=pltpu.VMEM)
    edge = shape((4, fields, lats), bf16)
    state, x_a, x_b = pl.pallas_call(
        forcing_kernel,
        in_specs=[pl.BlockSpec(memory_space=pltpu.SMEM), vmem, vmem, pl.BlockSpec(memory_space=pl.ANY)],
        out_specs=[vmem] * 3,
        out_shape=[shape((fields, lons, lats)), edge, edge],
        scratch_shapes=[
            pltpu.VMEM((fields, lons, lats), f32),
            pltpu.VMEM((fields * 9, lats), f32),
            pltpu.SemaphoreType.DMA,
        ],
        compiler_params=params(40),
        cost_estimate=cost(10**10, 2 * size),
        name="forcing",
    )(starts, lhs, places, adjoint_in.reshape(fields, lons, lats))

    whole_field = shape((tracers, levels, lons, lats))
    blocks = levels // LB
    note = shape((blocks, lons, 128), bf16)
    spread = jnp.asarray(edge_weights(), bf16)
    table = lat_weights()
    for step in range(STEPS):
        got_b = swap(x_b, "gx", False, True)
        got_a = swap(x_a, "gx", True, True)
        halves = pltpu.VMEM((tracers * LB * 16, 2 * lats), bf16)
        state = state.reshape(tracers, levels, lons, lats)
        partial = pl.pallas_call(
            inner_kernel,
            in_specs=[vmem] * 3,
            out_specs=[vmem] * 3,
            out_shape=[whole_field, note, note],
            scratch_shapes=[halves],
            compiler_params=params(24),
            cost_estimate=cost(5 * size, 2 * size),
            name="inner",
        )(state, courant_x, spread)
        zonal, to_a, to_b = pl.pallas_call(
            outer_kernel,
            in_specs=[vmem] * 8,
            out_specs=[vmem] * 3,
            out_shape=[whole_field, note, note],
            input_output_aliases={5: 0, 6: 1, 7: 2},
            scratch_shapes=[halves, pltpu.VMEM((tracers * LB * 33, lats), f32)],
            compiler_params=params(24),
            cost_estimate=cost(5 * size, 2 * size),
            name="outer",
        )(
            state,
            courant_x,
            spread,
            got_a.reshape(4, tracers, levels, lats),
            got_b.reshape(4, tracers, levels, lats),
            *partial,
        )
        y_b = swap(to_b, "gy", False, False)
        y_a = swap(to_a, "gy", True, False)
        inner = pl.pallas_call(
            lat_kernel,
            in_specs=[vmem] * 3,
            out_specs=vmem,
            out_shape=whole_field,
            scratch_shapes=[pltpu.VMEM((LB * tracers * lons, 2 * lats), bf16)],
            compiler_params=params(24),
            cost_estimate=cost(5 * size, 2 * size),
            name="lat",
        )(zonal, courant_y, jnp.asarray(table[:256], bf16))
        first = step == 0
        operands = [inner, courant_y, mixing, inv, q, y_a, y_b, jnp.asarray(table[256:], bf16)]
        out_shape = [whole_field, shape((tracers, lons, lats))]
        if first:
            out_shape += [edge, edge]
        else:
            operands.append(gradient)

        def kernel(*refs, first=first):
            column_kernel(first, *refs)

        out = pl.pallas_call(
            kernel,
            in_specs=[vmem] * len(operands),
            out_specs=[vmem] * len(out_shape),
            out_shape=out_shape,
            scratch_shapes=[pltpu.VMEM((levels * tracers * 8, 2 * lats), bf16)],
            compiler_params=params(24),
            cost_estimate=cost(5 * size, 2 * size),
            name="column",
        )(*operands)
        if first:
            state, gradient, x_a, x_b = out
        else:
            state, gradient = out
    return state, gradient


def solution(mesh):
    in_specs = (
        P(None, None, "gx", "gy"),
        P(None, "gx", "gy"),
        P(None, "gx", "gy"),
        P(None, "gx", "gy"),
        P(None, ("gx", "gy")),
        P(None, ("gx", "gy")),
        P(("gx", "gy")),
        P(("gx", "gy"), None),
    )
    out_specs = (P(None, None, "gx", "gy"), P(None, "gx", "gy"))
    return jax.shard_map(local, mesh=mesh, in_specs=in_specs, out_specs=out_specs, check_vma=False)
```

```python
import jax
import jax.numpy as jnp
import numpy as np
from jax import lax
from jax.experimental import pallas as pl
from jax.experimental.pallas import tpu as pltpu
from jax.sharding import PartitionSpec as P

STEPS = 2
LB = 8
CHUNK = 1024

D1, D2, D3 = 0.75, -0.15, 1.0 / 60.0
E1, E2, E3 = 1.5, -0.15, 1.0 / 90.0
E0 = -49.0 / 18.0

f32 = jnp.float32
bf16 = jnp.bfloat16


def fill_swap(table):
    row = lax.broadcasted_iota(jnp.int32, table.shape, 0)
    col = lax.broadcasted_iota(jnp.int32, table.shape, 1)
    want = ((col >> 5) & 3) * 128 + (col >> 7) * 32 + (col & 31)
    table[...] = jnp.where(row == want, 1.0, 0.0).astype(bf16)


def is_odd(axis):
    return (lax.axis_index(axis) & 1) == 1


def split(value):
    hi = value.astype(bf16)
    return hi, (value - hi.astype(f32)).astype(bf16)


def pack_kernel(counts, rows, weights, out, swap):
    step = pl.program_id(0)
    groups = rows.shape[1] // 128

    @pl.when(step == 0)
    def _():
        fill_swap(swap)

    lane = lax.broadcasted_iota(jnp.int32, (24, 128), 1)
    block = lane >> 5
    columns = [[] for _ in range(4)]
    for g in range(groups):
        lanes = slice(g * 128, g * 128 + 128)
        first = 4 * (step * groups + g)
        limit = jnp.where(
            block < 2,
            jnp.where(block == 0, counts[0, first], counts[0, first + 1]),
            jnp.where(block == 2, counts[0, first + 2], counts[0, first + 3]),
        )
        live = (lane & 31) < limit
        for q in range(3):
            columns[q].append(jnp.where(live, rows[24 * q : 24 * q + 24, lanes].astype(f32), 0.0))
        columns[3].append(jnp.concatenate([weights[:, lanes].astype(f32), jnp.zeros((20, 128), f32)], axis=0))
    wide = jnp.concatenate([jnp.concatenate(c, axis=0).astype(bf16) for c in columns], axis=1)
    moved = jnp.dot(wide, swap[...], preferred_element_type=f32)
    for g in range(groups):
        for i in range(4):
            out[4 * g + i] = moved[24 * g : 24 * g + 24, 128 * i : 128 * i + 128].astype(bf16)


def factor_kernel(mixing, inv_out, q_out):
    levels = inv_out.shape[0]
    top = mixing[0]
    inv = 1.0 / (1.0 + top)
    q = top * inv
    inv_out[0] = inv
    q_out[0] = q

    def level(l, carry):
        below, q = carry
        above = mixing[l]
        inv = 1.0 / (1.0 + below + above - below * q)
        q = above * inv
        inv_out[l] = inv
        q_out[l] = q
        return above, q

    below, q = lax.fori_loop(1, levels - 1, level, (top, q))
    inv_out[levels - 1] = 1.0 / (1.0 + below - below * q)
    q_out[levels - 1] = jnp.zeros_like(q)


def rank_kernel(bins, code, starts):
    piece = 256
    lane = lax.broadcasted_iota(jnp.int32, (piece, 128), 1)
    lane_f = lane.astype(f32)
    upto = (lax.broadcasted_iota(jnp.int32, (piece, piece), 1) <= lax.broadcasted_iota(jnp.int32, (piece, piece), 0))
    upto = jnp.where(upto, 1.0, 0.0).astype(bf16)
    row2 = lax.broadcasted_iota(jnp.int32, (256, 256), 0)
    col2 = lax.broadcasted_iota(jnp.int32, (256, 256), 1)
    spread = jnp.where((row2 >> 7) == (col2 >> 7), 1.0, 0.0).astype(bf16)
    ones = jnp.ones((8, CHUNK), bf16)
    for h in range(bins.shape[0] // CHUNK):
        own = bins[h * CHUNK : (h + 1) * CHUNK, :].astype(f32)
        wide = lax.broadcasted_iota(jnp.int32, own.shape, 1).astype(f32)
        below = jnp.where(own < wide, 1.0, 0.0).astype(bf16)
        start = jnp.dot(ones, below, preferred_element_type=f32)
        starts[8 * h : 8 * h + 8, :] = start.astype(jnp.int32)
        running = start[0:1, :] - 1.0
        for p in range(CHUNK // piece):
            at = slice(p * piece, p * piece + piece)
            mine = own[at] == lane_f
            one_hot = jnp.where(mine, 1.0, 0.0)
            place = jnp.dot(upto, one_hot.astype(bf16), preferred_element_type=f32) + running
            running = place[piece - 1 : piece, :]
            place = jnp.where(mine, place, 0.0)
            high = jnp.floor(place * (1.0 / 128.0))
            low = place - 128.0 * high
            both = jnp.dot(
                jnp.concatenate([high.astype(bf16), low.astype(bf16)], axis=1), spread, preferred_element_type=f32
            )
            found = jnp.where(both[:, 128:] == lane_f, both[:, :128], -1.0)
            code[h * CHUNK + p * piece : h * CHUNK + (p + 1) * piece, :] = found.astype(bf16)


def order_kernel(got, ids, code, lhs, places, swap, raw):
    half = lhs.shape[0] // 2
    slots = lhs.shape[1]
    fill_swap(swap)
    batch = 8
    for first in range(0, slots // 128, batch):
        wide = jnp.concatenate(
            [
                jnp.concatenate([got[4 * (first + g) + i].astype(f32) for g in range(batch)], axis=0).astype(bf16)
                for i in range(4)
            ],
            axis=1,
        )
        moved = jnp.dot(wide, swap[...], preferred_element_type=f32)
        for g in range(batch):
            lanes = slice((first + g) * 128, (first + g) * 128 + 128)
            for q in range(4):
                count = 24 if q < 3 else 8
                raw[24 * q : 24 * q + count, lanes] = moved[24 * g : 24 * g + count, 128 * q : 128 * q + 128]
    cells = ids[...]
    raw[76:77, :] = (cells & 127).astype(f32)
    raw[77:78, :] = (cells >> 7).astype(f32)
    one, zero = jnp.ones((), bf16), jnp.zeros((), bf16)
    for h in range(slots // CHUNK):
        block = raw[:, h * CHUNK : (h + 1) * CHUNK].astype(bf16)
        part = code[h * CHUNK : (h + 1) * CHUNK, :]
        for p in range(CHUNK // 256):
            one_hot = jnp.concatenate(
                [jnp.where(part == jnp.asarray(2 * p + a, bf16), one, zero) for a in range(2)], axis=1
            )
            done = jnp.dot(block, one_hot, preferred_element_type=f32)
            lanes = slice(h * CHUNK + p * 256, h * CHUNK + (p + 1) * 256)
            places[:, lanes] = done[72:80, :]
            for t in range(4):
                hi, lo = split(done[:72] * done[72 + t : 73 + t, :])
                lhs[72 * t : 72 * t + 72, lanes] = hi
                lhs[half + 72 * t : half + 72 * t + 72, lanes] = lo


def forcing_kernel(starts, lhs, places, adjoint_hbm, state, x_a, x_b, adjoint, turned, arrived):
    copy = pltpu.make_async_copy(adjoint_hbm, adjoint, arrived)
    copy.start()
    fields = state.shape[0]
    chunks = lhs.shape[1] // CHUNK
    last = CHUNK // 128 - 2
    steps = state.shape[1] // 8
    row = lax.broadcasted_iota(jnp.int32, (128, 256), 0).astype(f32)
    window = lax.broadcasted_iota(jnp.int32, (1, 256), 1)

    def placed(base, lon, skip):
        lat = places[4:5, pl.ds(base, 256)]
        slot_lon = places[5:6, pl.ds(base, 256)]
        if skip is not None:
            slot_lon = jnp.where(window >= skip, slot_lon, -1.0)
        return jnp.concatenate(
            [
                jnp.where(jnp.where(slot_lon == (lon + a).astype(f32), lat, -1.0) == row, 1.0, 0.0).astype(bf16)
                for a in range(2)
            ],
            axis=0,
        )

    def product(bases, one_hots):
        values = [lhs[at, pl.ds(base, 256)] for at in (slice(0, fields), slice(fields, 2 * fields)) for base in bases]
        return lax.dot_general(
            jnp.concatenate(values, axis=1),
            jnp.concatenate(one_hots * 2, axis=1),
            (((1,), (1,)), ((), ())),
            preferred_element_type=f32,
        )

    def extent(h, number):
        low = starts[8 * h, number]
        high = starts[8 * h, number + 1]
        first = jnp.minimum(low >> 7, last)
        return first, jnp.maximum(((high + 127) >> 7) - first - 1, 0) >> 1

    def eight(step, _):
        rest = jnp.int32(0)
        for pair in range(4):
            number = step * 4 + pair
            bases = []
            for h in range(chunks):
                first, visits = extent(h, number)
                rest = rest + visits
                bases.append(pl.multiple_of(h * CHUNK + first * 128, 128))
            total = product(bases, [placed(base, 2 * number, None) for base in bases])
            for a in range(2):
                turned[pl.ds(2 * pair + a, fields, stride=9), :] = total[:, 128 * a : 128 * a + 128]

        @pl.when(rest > 0)
        def _():
            def each(n, _):
                pair, h = n // chunks, n % chunks
                number = step * 4 + pair
                first, visits = extent(h, number)

                def more(j, _):
                    at = first + 2 + 2 * j
                    start = jnp.minimum(at, last)
                    base = pl.multiple_of(h * CHUNK + start * 128, 128)
                    both = product([base], [placed(base, 2 * number, (at - start) * 128)])
                    for a in range(2):
                        place = pl.ds(2 * pair + a, fields, stride=9)
                        turned[place, :] = turned[place, :] + both[:, 128 * a : 128 * a + 128]
                    return 0

                lax.fori_loop(0, visits, more, 0)
                return 0

            lax.fori_loop(0, 4 * chunks, each, 0)

        @pl.when(step == 0)
        def _():
            copy.wait()

        rows = pl.ds(pl.multiple_of(8 * step, 8), 8)
        for f in range(fields):
            cell = adjoint[f, rows, :] + turned[9 * f : 9 * f + 8, :]
            state[f, rows, :] = cell
            turned[9 * f : 9 * f + 8, :] = cell

        def edge(out, order):
            near, second, third = (turned[pl.ds(j, fields, stride=9), :] for j in order)
            out[0], out[1] = split(near)
            out[2] = second.astype(bf16)
            out[3] = third.astype(bf16)

        odd = is_odd("gx")
        for when, order, swapped in ((0, (0, 1, 2), odd), (steps - 1, (7, 6, 5), jnp.logical_not(odd))):
            for out, mine in ((x_a, swapped), (x_b, jnp.logical_not(swapped))):

                @pl.when((step == when) & mine)
                def _(out=out, order=order):
                    edge(out, order)

        return 0

    lax.fori_loop(0, steps, eight, 0)


def zonal_rows(outer, state, courant, courant_y, weights, halos, result, to_a, to_b, halves, kept, pad):
    lane = lax.broadcasted_iota(jnp.int32, (16, 128), 1)
    group = lane >> 2
    odd_x = is_odd("gx")
    odd_y = is_odd("gy")

    def block(b, _):
        levels = pl.ds(pl.multiple_of(b * LB, LB), LB)
        if outer:
            for t in range(4):
                parts = []
                for halo in halos:
                    part = [halo[n, t, levels, :].astype(f32) for n in range(4)]
                    parts.append((part[0] + part[1], part[2], part[3]))
                for side in range(2):
                    for k in range(3):
                        value = jnp.where(odd_x, parts[side][k], parts[1 - side][k])
                        pad[pl.ds(t * LB * 33 + (24 + k if side else 7 - k), LB, stride=33), :] = value
        notes = [jnp.zeros((16, 128), f32)] * 2
        for first in range(0, LB, 4):
            for l in range(first, first + 4):
                level = b * LB + l
                if outer:
                    c = jnp.concatenate([courant[level, 0:8, :], courant[level, 24:32, :]], axis=0)
                else:
                    c = courant[level, 8:24, :]
                factors = stencil_factors(c)
                for t in range(4):
                    if outer:
                        low = state[t, level, 0:8, :]
                        high = state[t, level, 24:32, :]
                        base = 33 * (t * LB + l)
                        pad[base + 8 : base + 16, :] = low
                        pad[base + 16 : base + 24, :] = high
                        v = {0: jnp.concatenate([low, high], axis=0)}
                        for k in (1, 2, 3):
                            v[-k] = jnp.concatenate(
                                [pad[base + 8 - k : base + 16 - k, :], state[t, level, 24 - k : 32 - k, :]], axis=0
                            )
                            v[k] = jnp.concatenate(
                                [state[t, level, k : 8 + k, :], pad[base + 16 + k : base + 24 + k, :]], axis=0
                            )
                    else:
                        v = {k: state[t, level, 8 + k : 24 + k, :] for k in range(-3, 4)}
                    out = v[0] * factors[0]
                    for k in (-1, 1, -2, 2, -3, 3):
                        out = out + v[k] * factors[k]
                    at = slice(16 * (4 * l + t), 16 * (4 * l + t) + 16)
                    if outer:
                        result[t, level] = out
                    else:
                        kept[at, :] = out
                    halves[at, 0:128], halves[at, 128:256] = split(out)
            at = slice(64 * first, 64 * first + 256)
            edges = jnp.dot(halves[at, :], weights[...], preferred_element_type=f32)
            for l in range(4):
                if not outer:
                    level = b * LB + first + l
                    rows = slice(64 * l, 64 * l + 64)
                    kept_rows = slice(64 * (first + l), 64 * (first + l) + 64)
                    part = edges[rows, 256:512].reshape(4, 16, 256)
                    c = courant_y[level, 8:24, :]
                    result[:, level, 8:24, :] = (
                        kept[kept_rows, :].reshape(4, 16, 128)
                        + (c * (1.0 / 60.0)) * part[:, :, :128]
                        + (c * c * (1.0 / 360.0)) * part[:, :, 128:]
                    )
                for t in range(4):
                    mine = group == t * LB + first + l
                    rows = slice(16 * (4 * l + t), 16 * (4 * l + t) + 16)
                    notes = [jnp.where(mine, edges[rows, 128 * n : 128 * n + 128], notes[n]) for n in range(2)]
        for out, note in (
            (to_a, jnp.where(odd_y, notes[0], notes[1]).astype(bf16)),
            (to_b, jnp.where(odd_y, notes[1], notes[0]).astype(bf16)),
        ):
            if outer:
                out[b, 0:8] = note[:8]
                out[b, 24:32] = note[8:]
            else:
                out[b, 8:24] = note
        return 0

    lax.fori_loop(0, courant.shape[0] // LB, block, 0)


def inner_kernel(state, courant, courant_y, weights, result, to_a, to_b, halves, kept):
    zonal_rows(False, state, courant, courant_y, weights, None, result, to_a, to_b, halves, kept, None)


def outer_kernel(state, courant, weights, from_a, from_b, _a, _b, zonal, to_a, to_b, halves, pad):
    zonal_rows(True, state, courant, None, weights, (from_a, from_b), zonal, to_a, to_b, halves, None, pad)


def stencil_factors(c):
    c2 = 0.5 * c * c
    factors = {0: 1.0 + E0 * c2}
    for k, d, e in ((1, D1, E1), (2, D2, E2), (3, D3, E3)):
        slope, curve = d * c, e * c2
        factors[k] = curve + slope
        factors[-k] = curve - slope
    return factors


def lat_kernel(zonal, courant, weights, _result, result, halves):
    tracers, levels, lons, lats = zonal.shape
    rows = tracers * lons

    def block(b, _):
        for l in range(LB):
            level = b * LB + l
            at = slice(l * rows, (l + 1) * rows)
            halves[at, 0:128], halves[at, 128:256] = split(zonal[:, level].reshape(rows, lats))
        for l in range(0, LB, 4):
            at = slice(l * rows, (l + 4) * rows)
            several = jnp.dot(halves[at, :], weights[...], preferred_element_type=f32)
            for n in range(4):
                level = b * LB + l + n
                both = several[n * rows : (n + 1) * rows].reshape(tracers, lons, 256)
                c = jnp.concatenate([courant[level, 0:8, :], courant[level, 24:32, :]], axis=0)
                out = (
                    zonal[:, level]
                    + (c * (1.0 / 60.0)) * both[:, :, :128]
                    + (c * c * (1.0 / 360.0)) * both[:, :, 128:]
                )
                result[:, level, 0:8, :] = out[:, :8]
                result[:, level, 24:32, :] = out[:, 8:]
        return 0

    lax.fori_loop(0, levels // LB, block, 0)


def column_kernel(first, inner, courant, mixing, inv, q, from_a, from_b, weights, *rest):
    lhs = rest[-1]
    if first:
        state, gradient, x_a, x_b = rest[:-1]
    else:
        before, state, gradient = rest[:-1]
    levels = inv.shape[0]
    lons = 32
    rows = 4 * lons
    lane = lax.broadcasted_iota(jnp.int32, (rows, 128), 1)
    row = lax.broadcasted_iota(jnp.int32, (rows, 128), 0)
    owner = ((lane >> 2) - (row >> 5) * LB).astype(f32).astype(bf16)
    zero = jnp.zeros((), bf16)
    odd_y = is_odd("gy")

    def tile(r, _):
        here = pl.ds(pl.multiple_of(lons * r, lons), lons)
        carry = None
        for b in range(levels // LB):
            a, z = from_a[b, here, :].astype(f32), from_b[b, here, :].astype(f32)
            notes = [
                jnp.concatenate([note] * 4, axis=0).astype(bf16)
                for note in (jnp.where(odd_y, a, z), jnp.where(odd_y, z, a))
            ]
            for l in range(LB):
                at = slice((b * LB + l) * rows, (b * LB + l + 1) * rows)
                mine = owner == jnp.asarray(l, bf16)
                lhs[at, 0:128] = jnp.where(mine, notes[0], zero)
                lhs[at, 128:256] = jnp.where(mine, notes[1], zero)
            both = jnp.dot(
                lhs[b * LB * rows : (b + 1) * LB * rows, :], weights[...], preferred_element_type=f32
            )
            for l in range(LB):
                level = b * LB + l
                c = courant[level, here, :]
                part = both[l * rows : l * rows + rows].reshape(4, lons, 256)
                y = inner[:, level, here, :]
                y = y + (c * (1.0 / 60.0)) * part[:, :, :128] + (c * c * (1.0 / 360.0)) * part[:, :, 128:]
                if level > 0:
                    y = y + mixing[level - 1, here, :] * carry
                carry = y * inv[level, here, :]
                state[:, level, here, :] = carry

        def back(j, carry):
            level = levels - 2 - j
            carry = state[:, level, here, :] + q[level, here, :] * carry
            state[:, level, here, :] = carry
            return carry

        carry = lax.fori_loop(0, levels - 1, back, carry, unroll=8)
        gradient[:, here, :] = carry if first else before[:, here, :] + carry
        return 0

    lax.fori_loop(0, inner.shape[2] // lons, tile, 0)
    if first:

        def edge(out, order):
            for t in range(4):
                rows = slice(levels * t, levels * t + levels)
                near, second, third = (state[t, :, j, :] for j in order)
                out[0, rows], out[1, rows] = split(near)
                out[2, rows] = second.astype(bf16)
                out[3, rows] = third.astype(bf16)

        low, high = (0, 1, 2), (31, 30, 29)

        @pl.when(is_odd("gx"))
        def _():
            edge(x_a, low)
            edge(x_b, high)

        @pl.when(jnp.logical_not(is_odd("gx")))
        def _():
            edge(x_a, high)
            edge(x_b, low)


def edge_weights():
    table = np.zeros((256, 256), np.float32)
    for lane in range(128):
        part = lane % 4
        table[(128, part)[part < 3], lane] = 1
        table[(255, 125 + part)[part < 3], 128 + lane] = 1
    return table


def lat_weights():
    first = {1: 45, 2: -9, 3: 1}
    second = {0: -490, 1: 270, 2: -27, 3: 2}
    table = np.zeros((512, 256), np.float32)

    def fill(row, place):
        for out in range(128):
            k = place - out
            if abs(k) <= 3:
                table[row, out] = first.get(abs(k), 0) * (1 if k > 0 else -1)
                table[row, 128 + out] = second[abs(k)]

    for lane in range(128):
        fill(lane, lane)
        fill(128 + lane, lane)
        fill(256 + lane, (-3, -2, -1, -1)[lane % 4])
        fill(384 + lane, (128, 129, 130, 128)[lane % 4])
    return table


def cost(flops, size):
    return pl.CostEstimate(flops=flops, bytes_accessed=size, transcendentals=0)


def params(mib):
    return pltpu.CompilerParams(vmem_limit_bytes=mib * 2**20)


def shape(dims, kind=f32):
    return jax.ShapeDtypeStruct(dims, kind)


def swap(value, axis, first, closed):
    count = lax.axis_size(axis)
    pairs = []
    for low in range(0 if first else 1, count, 2):
        if low + 1 < count or closed:
            high = (low + 1) % count
            pairs += [(low, high), (high, low)]
    return lax.ppermute(value, axis, pairs)


def local(adjoint_in, courant_x, courant_y, mixing, kernel_rows, tracer_weights, column_ids, counts):
    tracers, levels, lons, lats = adjoint_in.shape
    devices = lax.axis_size(("gx", "gy"))
    slots = kernel_rows.shape[1]
    fields = tracers * levels
    size = fields * lons * lats * 4

    packed = pl.pallas_call(
        pack_kernel,
        grid=(2,),
        in_specs=[
            pl.BlockSpec(memory_space=pltpu.SMEM),
            pl.BlockSpec((levels, slots // 2), lambda i: (0, i)),
            pl.BlockSpec((tracers, slots // 2), lambda i: (0, i)),
        ],
        out_specs=pl.BlockSpec((devices // 2, 24, 128), lambda i: (i, 0, 0)),
        out_shape=shape((devices, 24, 128), bf16),
        scratch_shapes=[pltpu.VMEM((512, 512), bf16)],
        compiler_params=params(60),
        name="pack",
    )(counts, kernel_rows, tracer_weights)
    got = lax.all_to_all(packed, ("gx", "gy"), split_axis=0, concat_axis=0, tiled=True)

    inv, q = pl.pallas_call(
        factor_kernel,
        out_shape=[shape((levels, lons, lats))] * 2,
        compiler_params=params(16),
        cost_estimate=cost(30 * levels * lons * lats, 3 * levels * lons * lats * 4),
        name="factor",
    )(mixing)
    bins = jnp.broadcast_to((column_ids // (2 * lats)).astype(bf16)[:, None], (slots, 128))
    code, starts = pl.pallas_call(
        rank_kernel,
        out_shape=[shape((slots, 128), bf16), shape((8 * (slots // CHUNK), 128), jnp.int32)],
        compiler_params=params(16),
        cost_estimate=cost(10**9, 2 * 10**6),
        name="rank",
    )(bins)
    lhs, places = pl.pallas_call(
        order_kernel,
        out_shape=[shape((2 * fields, slots), bf16), shape((8, slots))],
        scratch_shapes=[pltpu.VMEM((512, 512), bf16), pltpu.VMEM((80, slots), f32)],
        compiler_params=params(24),
        cost_estimate=cost(10**9, 8 * 10**6),
        name="order",
    )(got, column_ids.reshape(1, slots), code)

    vmem = pl.BlockSpec(memory_space=pltpu.VMEM)
    edge = shape((4, fields, lats), bf16)
    state, x_a, x_b = pl.pallas_call(
        forcing_kernel,
        in_specs=[pl.BlockSpec(memory_space=pltpu.SMEM), vmem, vmem, pl.BlockSpec(memory_space=pl.ANY)],
        out_specs=[vmem] * 3,
        out_shape=[shape((fields, lons, lats)), edge, edge],
        scratch_shapes=[
            pltpu.VMEM((fields, lons, lats), f32),
            pltpu.VMEM((fields * 9, lats), f32),
            pltpu.SemaphoreType.DMA,
        ],
        compiler_params=params(40),
        cost_estimate=cost(10**10, 2 * size),
        name="forcing",
    )(starts, lhs, places, adjoint_in.reshape(fields, lons, lats))

    whole_field = shape((tracers, levels, lons, lats))
    blocks = levels // LB
    note = shape((blocks, lons, 128), bf16)
    spread = edge_weights()
    table = lat_weights()
    for step in range(STEPS):
        got_b = swap(x_b, "gx", False, True)
        got_a = swap(x_a, "gx", True, True)
        halves = pltpu.VMEM((tracers * LB * 16, 2 * lats), bf16)
        state = state.reshape(tracers, levels, lons, lats)
        result, to_a, to_b = pl.pallas_call(
            inner_kernel,
            in_specs=[vmem] * 4,
            out_specs=[vmem] * 3,
            out_shape=[whole_field, note, note],
            scratch_shapes=[halves, pltpu.VMEM((tracers * LB * 16, lats), f32)],
            compiler_params=params(24),
            cost_estimate=cost(5 * size, 2 * size),
            name="inner",
        )(state, courant_x, courant_y, jnp.asarray(np.concatenate([spread, table[:256]], axis=1), bf16))
        zonal, to_a, to_b = pl.pallas_call(
            outer_kernel,
            in_specs=[vmem] * 7,
            out_specs=[vmem] * 3,
            out_shape=[shape((tracers, levels, 16, lats)), note, note],
            input_output_aliases={5: 1, 6: 2},
            scratch_shapes=[halves, pltpu.VMEM((tracers * LB * 33, lats), f32)],
            compiler_params=params(24),
            cost_estimate=cost(5 * size, 2 * size),
            name="outer",
        )(
            state,
            courant_x,
            jnp.asarray(spread, bf16),
            got_a.reshape(4, tracers, levels, lats),
            got_b.reshape(4, tracers, levels, lats),
            to_a,
            to_b,
        )
        y_b = swap(to_b, "gy", False, False)
        y_a = swap(to_a, "gy", True, False)
        inner = pl.pallas_call(
            lat_kernel,
            in_specs=[vmem] * 4,
            out_specs=vmem,
            out_shape=whole_field,
            input_output_aliases={3: 0},
            scratch_shapes=[halves],
            compiler_params=params(24),
            cost_estimate=cost(5 * size, 2 * size),
            name="lat",
        )(zonal, courant_y, jnp.asarray(table[:256], bf16), result)
        first = step == 0
        operands = [inner, courant_y, mixing, inv, q, y_a, y_b, jnp.asarray(table[256:], bf16)]
        out_shape = [whole_field, shape((tracers, lons, lats))]
        if first:
            out_shape += [edge, edge]
        else:
            operands.append(gradient)

        def kernel(*refs, first=first):
            column_kernel(first, *refs)

        out = pl.pallas_call(
            kernel,
            in_specs=[vmem] * len(operands),
            out_specs=[vmem] * len(out_shape),
            out_shape=out_shape,
            scratch_shapes=[pltpu.VMEM((levels * tracers * 32, 2 * lats), bf16)],
            compiler_params=params(24),
            cost_estimate=cost(5 * size, 2 * size),
            name="column",
        )(*operands)
        if first:
            state, gradient, x_a, x_b = out
        else:
            state, gradient = out
    return state, gradient


def solution(mesh):
    in_specs = (
        P(None, None, "gx", "gy"),
        P(None, "gx", "gy"),
        P(None, "gx", "gy"),
        P(None, "gx", "gy"),
        P(None, ("gx", "gy")),
        P(None, ("gx", "gy")),
        P(("gx", "gy")),
        P(("gx", "gy"), None),
    )
    out_specs = (P(None, None, "gx", "gy"), P(None, "gx", "gy"))
    return jax.shard_map(local, mesh=mesh, in_specs=in_specs, out_specs=out_specs, check_vma=False)
```

```python
import jax
import jax.numpy as jnp
import numpy as np
from jax import lax
from jax.experimental import pallas as pl
from jax.experimental.pallas import tpu as pltpu
from jax.sharding import PartitionSpec as P

STEPS = 2
LB = 8
CHUNK = 1024

D1, D2, D3 = 0.75, -0.15, 1.0 / 60.0
E1, E2, E3 = 1.5, -0.15, 1.0 / 90.0
E0 = -49.0 / 18.0

f32 = jnp.float32
bf16 = jnp.bfloat16


def fill_swap(table):
    row = lax.broadcasted_iota(jnp.int32, table.shape, 0)
    col = lax.broadcasted_iota(jnp.int32, table.shape, 1)
    want = ((col >> 5) & 3) * 128 + (col >> 7) * 32 + (col & 31)
    table[...] = jnp.where(row == want, 1.0, 0.0).astype(bf16)


def is_odd(axis):
    return (lax.axis_index(axis) & 1) == 1


def split(value):
    hi = value.astype(bf16)
    return hi, (value - hi.astype(f32)).astype(bf16)


def pack_kernel(counts, rows, weights, out, swap):
    step = pl.program_id(0)
    groups = rows.shape[1] // 128

    @pl.when(step == 0)
    def _():
        fill_swap(swap)

    lane = lax.broadcasted_iota(jnp.int32, (24, 128), 1)
    block = lane >> 5
    columns = [[] for _ in range(4)]
    for g in range(groups):
        lanes = slice(g * 128, g * 128 + 128)
        first = 4 * (step * groups + g)
        limit = jnp.where(
            block < 2,
            jnp.where(block == 0, counts[0, first], counts[0, first + 1]),
            jnp.where(block == 2, counts[0, first + 2], counts[0, first + 3]),
        )
        live = (lane & 31) < limit
        for q in range(3):
            columns[q].append(jnp.where(live, rows[24 * q : 24 * q + 24, lanes].astype(f32), 0.0))
        columns[3].append(jnp.concatenate([weights[:, lanes].astype(f32), jnp.zeros((20, 128), f32)], axis=0))
    wide = jnp.concatenate([jnp.concatenate(c, axis=0).astype(bf16) for c in columns], axis=1)
    moved = jnp.dot(wide, swap[...], preferred_element_type=f32)
    for g in range(groups):
        for i in range(4):
            out[4 * g + i] = moved[24 * g : 24 * g + 24, 128 * i : 128 * i + 128].astype(bf16)


def factor_kernel(mixing, inv_out, q_out):
    levels = inv_out.shape[0]
    top = mixing[0]
    inv = 1.0 / (1.0 + top)
    q = top * inv
    inv_out[0] = inv
    q_out[0] = q

    def level(l, carry):
        below, q = carry
        above = mixing[l]
        inv = 1.0 / (1.0 + below + above - below * q)
        q = above * inv
        inv_out[l] = inv
        q_out[l] = q
        return above, q

    below, q = lax.fori_loop(1, levels - 1, level, (top, q))
    inv_out[levels - 1] = 1.0 / (1.0 + below - below * q)
    q_out[levels - 1] = jnp.zeros_like(q)


def rank_kernel(bins, code, starts):
    piece = 256
    lane = lax.broadcasted_iota(jnp.int32, (piece, 128), 1)
    lane_f = lane.astype(f32)
    upto = (lax.broadcasted_iota(jnp.int32, (piece, piece), 1) <= lax.broadcasted_iota(jnp.int32, (piece, piece), 0))
    upto = jnp.where(upto, 1.0, 0.0).astype(bf16)
    row2 = lax.broadcasted_iota(jnp.int32, (256, 256), 0)
    col2 = lax.broadcasted_iota(jnp.int32, (256, 256), 1)
    spread = jnp.where((row2 >> 7) == (col2 >> 7), 1.0, 0.0).astype(bf16)
    ones = jnp.ones((8, CHUNK), bf16)
    for h in range(bins.shape[0] // CHUNK):
        own = bins[h * CHUNK : (h + 1) * CHUNK, :].astype(f32)
        wide = lax.broadcasted_iota(jnp.int32, own.shape, 1).astype(f32)
        below = jnp.where(own < wide, 1.0, 0.0).astype(bf16)
        start = jnp.dot(ones, below, preferred_element_type=f32)
        starts[8 * h : 8 * h + 8, :] = start.astype(jnp.int32)
        running = start[0:1, :] - 1.0
        for p in range(CHUNK // piece):
            at = slice(p * piece, p * piece + piece)
            mine = own[at] == lane_f
            one_hot = jnp.where(mine, 1.0, 0.0)
            place = jnp.dot(upto, one_hot.astype(bf16), preferred_element_type=f32) + running
            running = place[piece - 1 : piece, :]
            place = jnp.where(mine, place, 0.0)
            high = jnp.floor(place * (1.0 / 128.0))
            low = place - 128.0 * high
            both = jnp.dot(
                jnp.concatenate([high.astype(bf16), low.astype(bf16)], axis=1), spread, preferred_element_type=f32
            )
            found = jnp.where(both[:, 128:] == lane_f, both[:, :128], -1.0)
            code[h * CHUNK + p * piece : h * CHUNK + (p + 1) * piece, :] = found.astype(bf16)


def order_kernel(got, ids, code, lhs, places, swap, raw):
    half = lhs.shape[0] // 2
    slots = lhs.shape[1]
    fill_swap(swap)
    batch = 8
    for first in range(0, slots // 128, batch):
        wide = jnp.concatenate(
            [
                jnp.concatenate([got[4 * (first + g) + i].astype(f32) for g in range(batch)], axis=0).astype(bf16)
                for i in range(4)
            ],
            axis=1,
        )
        moved = jnp.dot(wide, swap[...], preferred_element_type=f32)
        for g in range(batch):
            lanes = slice((first + g) * 128, (first + g) * 128 + 128)
            for q in range(4):
                count = 24 if q < 3 else 8
                raw[24 * q : 24 * q + count, lanes] = moved[24 * g : 24 * g + count, 128 * q : 128 * q + 128]
    cells = ids[...]
    raw[76:77, :] = (cells & 127).astype(f32)
    raw[77:78, :] = (cells >> 7).astype(f32)
    one, zero = jnp.ones((), bf16), jnp.zeros((), bf16)
    for h in range(slots // CHUNK):
        block = raw[:, h * CHUNK : (h + 1) * CHUNK].astype(bf16)
        part = code[h * CHUNK : (h + 1) * CHUNK, :]
        for p in range(CHUNK // 256):
            one_hot = jnp.concatenate(
                [jnp.where(part == jnp.asarray(2 * p + a, bf16), one, zero) for a in range(2)], axis=1
            )
            done = jnp.dot(block, one_hot, preferred_element_type=f32)
            lanes = slice(h * CHUNK + p * 256, h * CHUNK + (p + 1) * 256)
            places[:, lanes] = done[72:80, :]
            for t in range(4):
                hi, lo = split(done[:72] * done[72 + t : 73 + t, :])
                lhs[72 * t : 72 * t + 72, lanes] = hi
                lhs[half + 72 * t : half + 72 * t + 72, lanes] = lo


def forcing_kernel(outer, starts, lhs, places, adjoint_hbm, *rest):
    if outer:
        state, x_a, x_b, adjoint, turned, arrived = rest
        order = (0, 3)
    else:
        _, state, adjoint, turned, arrived = rest
        order = (1, 2)
    copies = [
        pltpu.make_async_copy(adjoint_hbm.at[:, pl.ds(8 * step, 8), :], adjoint.at[n], arrived.at[n])
        for n, step in enumerate(order)
    ]
    for copy in copies:
        copy.start()
    fields = state.shape[0]
    chunks = lhs.shape[1] // CHUNK
    last = CHUNK // 128 - 2
    row = lax.broadcasted_iota(jnp.int32, (128, 256), 0).astype(f32)
    window = lax.broadcasted_iota(jnp.int32, (1, 256), 1)

    def placed(base, lon, skip):
        lat = places[4:5, pl.ds(base, 256)]
        slot_lon = places[5:6, pl.ds(base, 256)]
        if skip is not None:
            slot_lon = jnp.where(window >= skip, slot_lon, -1.0)
        return jnp.concatenate(
            [
                jnp.where(jnp.where(slot_lon == (lon + a).astype(f32), lat, -1.0) == row, 1.0, 0.0).astype(bf16)
                for a in range(2)
            ],
            axis=0,
        )

    def product(bases, one_hots):
        values = [lhs[at, pl.ds(base, 256)] for at in (slice(0, fields), slice(fields, 2 * fields)) for base in bases]
        return lax.dot_general(
            jnp.concatenate(values, axis=1),
            jnp.concatenate(one_hots * 2, axis=1),
            (((1,), (1,)), ((), ())),
            preferred_element_type=f32,
        )

    def extent(h, number):
        low = starts[8 * h, number]
        high = starts[8 * h, number + 1]
        first = jnp.minimum(low >> 7, last)
        return first, jnp.maximum(((high + 127) >> 7) - first - 1, 0) >> 1

    def eight(n, _):
        step = order[0] + n * (order[1] - order[0])
        rest = jnp.int32(0)
        for pair in range(4):
            number = step * 4 + pair
            bases = []
            for h in range(chunks):
                first, visits = extent(h, number)
                rest = rest + visits
                bases.append(pl.multiple_of(h * CHUNK + first * 128, 128))
            total = product(bases, [placed(base, 2 * number, None) for base in bases])
            for a in range(2):
                turned[pl.ds(2 * pair + a, fields, stride=9), :] = total[:, 128 * a : 128 * a + 128]

        @pl.when(rest > 0)
        def _():
            def each(n, _):
                pair, h = n // chunks, n % chunks
                number = step * 4 + pair
                first, visits = extent(h, number)

                def more(j, _):
                    at = first + 2 + 2 * j
                    start = jnp.minimum(at, last)
                    base = pl.multiple_of(h * CHUNK + start * 128, 128)
                    both = product([base], [placed(base, 2 * number, (at - start) * 128)])
                    for a in range(2):
                        place = pl.ds(2 * pair + a, fields, stride=9)
                        turned[place, :] = turned[place, :] + both[:, 128 * a : 128 * a + 128]
                    return 0

                lax.fori_loop(0, visits, more, 0)
                return 0

            lax.fori_loop(0, 4 * chunks, each, 0)

        for k in range(2):

            @pl.when(n == k)
            def _(k=k):
                copies[k].wait()

        rows = pl.ds(pl.multiple_of(8 * step, 8), 8)
        for f in range(fields):
            cell = adjoint[n, f] + turned[9 * f : 9 * f + 8, :]
            state[f, rows, :] = cell
            turned[9 * f : 9 * f + 8, :] = cell

        def edge(out, order):
            near, second, third = (turned[pl.ds(j, fields, stride=9), :] for j in order)
            out[0], out[1] = split(near)
            out[2] = second.astype(bf16)
            out[3] = third.astype(bf16)

        if outer:
            odd = is_odd("gx")
            for when, sides, swapped in ((0, (0, 1, 2), odd), (1, (7, 6, 5), jnp.logical_not(odd))):
                for out, mine in ((x_a, swapped), (x_b, jnp.logical_not(swapped))):

                    @pl.when((n == when) & mine)
                    def _(out=out, sides=sides):
                        edge(out, sides)

        return 0

    lax.fori_loop(0, 2, eight, 0)


def zonal_rows(outer, state, courant, spread, halos, zonal, to_a, to_b, halves, pad):
    lane = lax.broadcasted_iota(jnp.int32, (16, 128), 1)
    group = lane >> 2
    odd_x = is_odd("gx")
    odd_y = is_odd("gy")

    def block(b, _):
        levels = pl.ds(pl.multiple_of(b * LB, LB), LB)
        if outer:
            for t in range(4):
                parts = []
                for halo in halos:
                    part = [halo[n, t, levels, :].astype(f32) for n in range(4)]
                    parts.append((part[0] + part[1], part[2], part[3]))
                for side in range(2):
                    for k in range(3):
                        value = jnp.where(odd_x, parts[side][k], parts[1 - side][k])
                        pad[pl.ds(t * LB * 33 + (24 + k if side else 7 - k), LB, stride=33), :] = value
        notes = [jnp.zeros((16, 128), f32)] * 2
        for first in range(0, LB, 4):
            for l in range(first, first + 4):
                level = b * LB + l
                if outer:
                    c = jnp.concatenate([courant[level, 0:8, :], courant[level, 24:32, :]], axis=0)
                else:
                    c = courant[level, 8:24, :]
                factors = stencil_factors(c)
                for t in range(4):
                    if outer:
                        low = state[t, level, 0:8, :]
                        high = state[t, level, 24:32, :]
                        base = 33 * (t * LB + l)
                        pad[base + 8 : base + 16, :] = low
                        pad[base + 16 : base + 24, :] = high
                        v = {0: jnp.concatenate([low, high], axis=0)}
                        for k in (1, 2, 3):
                            v[-k] = jnp.concatenate(
                                [pad[base + 8 - k : base + 16 - k, :], state[t, level, 24 - k : 32 - k, :]], axis=0
                            )
                            v[k] = jnp.concatenate(
                                [state[t, level, k : 8 + k, :], pad[base + 16 + k : base + 24 + k, :]], axis=0
                            )
                    else:
                        v = {k: state[t, level, 8 + k : 24 + k, :] for k in range(-3, 4)}
                    out = v[0] * factors[0]
                    for k in (-1, 1, -2, 2, -3, 3):
                        out = out + v[k] * factors[k]
                    if outer:
                        zonal[t, level, 0:8, :] = out[:8]
                        zonal[t, level, 24:32, :] = out[8:]
                    else:
                        zonal[t, level, 8:24, :] = out
                    at = slice(16 * (4 * l + t), 16 * (4 * l + t) + 16)
                    halves[at, 0:128], halves[at, 128:256] = split(out)
            at = slice(64 * first, 64 * first + 256)
            edges = jnp.dot(halves[at, :], spread[...], preferred_element_type=f32)
            for l in range(4):
                for t in range(4):
                    mine = group == t * LB + first + l
                    rows = slice(16 * (4 * l + t), 16 * (4 * l + t) + 16)
                    notes = [jnp.where(mine, edges[rows, 128 * n : 128 * n + 128], notes[n]) for n in range(2)]
        for out, note in (
            (to_a, jnp.where(odd_y, notes[0], notes[1]).astype(bf16)),
            (to_b, jnp.where(odd_y, notes[1], notes[0]).astype(bf16)),
        ):
            if outer:
                out[b, 0:8] = note[:8]
                out[b, 24:32] = note[8:]
            else:
                out[b, 8:24] = note
        return 0

    lax.fori_loop(0, courant.shape[0] // LB, block, 0)


def inner_kernel(state, courant, spread, zonal, to_a, to_b, halves):
    zonal_rows(False, state, courant, spread, None, zonal, to_a, to_b, halves, None)


def outer_kernel(state, courant, spread, from_a, from_b, _z, _a, _b, zonal, to_a, to_b, halves, pad):
    zonal_rows(True, state, courant, spread, (from_a, from_b), zonal, to_a, to_b, halves, pad)


def stencil_factors(c):
    c2 = 0.5 * c * c
    factors = {0: 1.0 + E0 * c2}
    for k, d, e in ((1, D1, E1), (2, D2, E2), (3, D3, E3)):
        slope, curve = d * c, e * c2
        factors[k] = curve + slope
        factors[-k] = curve - slope
    return factors


def lat_kernel(zonal, courant, weights, result, halves):
    tracers, levels, lons, lats = zonal.shape
    rows = tracers * lons

    def block(b, _):
        for l in range(LB):
            level = b * LB + l
            at = slice(l * rows, (l + 1) * rows)
            halves[at, 0:128], halves[at, 128:256] = split(zonal[:, level].reshape(rows, lats))
        for l in range(LB):
            level = b * LB + l
            at = slice(l * rows, (l + 1) * rows)
            both = jnp.dot(halves[at, :], weights[...], preferred_element_type=f32).reshape(tracers, lons, 256)
            c = courant[level]
            result[:, level] = (
                zonal[:, level] + (c * (1.0 / 60.0)) * both[:, :, :128] + (c * c * (1.0 / 360.0)) * both[:, :, 128:]
            )
        return 0

    lax.fori_loop(0, levels // LB, block, 0)


def column_kernel(pieces, first, inner, courant, mixing, inv, q, from_a, from_b, weights, *rest):
    lhs = rest[-1]
    x_a = x_b = before = None
    if not first:
        before, state, gradient = rest[:-1]
    elif len(pieces) == 2:
        state, gradient, x_a, x_b = rest[:-1]
    else:
        _, _, state, gradient = rest[:-1]
    levels = inv.shape[0]
    lons = sum(count for _, count in pieces)
    rows = 4 * lons

    def get(ref, *index):
        parts = [ref[(*index, slice(start, start + count), slice(None))] for start, count in pieces]
        return parts[0] if len(parts) == 1 else jnp.concatenate(parts, axis=-2)

    def put(ref, value, *index):
        done = 0
        for start, count in pieces:
            ref[(*index, slice(start, start + count), slice(None))] = value[..., done : done + count, :]
            done += count

    lane = lax.broadcasted_iota(jnp.int32, (rows, 128), 1)
    row = lax.broadcasted_iota(jnp.int32, (rows, 128), 0)
    owner = ((lane >> 2) - (row // lons) * LB).astype(f32).astype(bf16)
    zero = jnp.zeros((), bf16)
    odd_y = is_odd("gy")

    every = slice(None)
    carry = None
    for b in range(levels // LB):
        a, z = get(from_a, b).astype(f32), get(from_b, b).astype(f32)
        notes = [
            jnp.concatenate([note] * 4, axis=0).astype(bf16) for note in (jnp.where(odd_y, a, z), jnp.where(odd_y, z, a))
        ]
        for l in range(LB):
            at = slice((b * LB + l) * rows, (b * LB + l + 1) * rows)
            mine = owner == jnp.asarray(l, bf16)
            lhs[at, 0:128] = jnp.where(mine, notes[0], zero)
            lhs[at, 128:256] = jnp.where(mine, notes[1], zero)
        both = jnp.dot(lhs[b * LB * rows : (b + 1) * LB * rows, :], weights[...], preferred_element_type=f32)
        for l in range(LB):
            level = b * LB + l
            c = get(courant, level)
            part = both[l * rows : l * rows + rows].reshape(4, lons, 256)
            y = get(inner, every, level)
            y = y + (c * (1.0 / 60.0)) * part[:, :, :128] + (c * c * (1.0 / 360.0)) * part[:, :, 128:]
            if level > 0:
                y = y + get(mixing, level - 1) * carry
            carry = y * get(inv, level)
            put(state, carry, every, level)

    def back(j, carry):
        level = levels - 2 - j
        carry = get(state, every, level) + get(q, level) * carry
        put(state, carry, every, level)
        return carry

    carry = lax.fori_loop(0, levels - 1, back, carry, unroll=8)
    put(gradient, carry if first else get(before, every) + carry, every)
    if x_a is not None:

        def edge(out, order):
            for t in range(4):
                rows = slice(levels * t, levels * t + levels)
                near, second, third = (state[t, :, j, :] for j in order)
                out[0, rows], out[1, rows] = split(near)
                out[2, rows] = second.astype(bf16)
                out[3, rows] = third.astype(bf16)

        low, high = (0, 1, 2), (31, 30, 29)

        @pl.when(is_odd("gx"))
        def _():
            edge(x_a, low)
            edge(x_b, high)

        @pl.when(jnp.logical_not(is_odd("gx")))
        def _():
            edge(x_a, high)
            edge(x_b, low)


def edge_weights():
    table = np.zeros((256, 256), np.float32)
    for lane in range(128):
        part = lane % 4
        table[(128, part)[part < 3], lane] = 1
        table[(255, 125 + part)[part < 3], 128 + lane] = 1
    return table


def lat_weights():
    first = {1: 45, 2: -9, 3: 1}
    second = {0: -490, 1: 270, 2: -27, 3: 2}
    table = np.zeros((512, 256), np.float32)

    def fill(row, place):
        for out in range(128):
            k = place - out
            if abs(k) <= 3:
                table[row, out] = first.get(abs(k), 0) * (1 if k > 0 else -1)
                table[row, 128 + out] = second[abs(k)]

    for lane in range(128):
        fill(lane, lane)
        fill(128 + lane, lane)
        fill(256 + lane, (-3, -2, -1, -1)[lane % 4])
        fill(384 + lane, (128, 129, 130, 128)[lane % 4])
    return table


def cost(flops, size):
    return pl.CostEstimate(flops=flops, bytes_accessed=size, transcendentals=0)


def params(mib):
    return pltpu.CompilerParams(vmem_limit_bytes=mib * 2**20)


def shape(dims, kind=f32):
    return jax.ShapeDtypeStruct(dims, kind)


def swap(value, axis, first, closed):
    count = lax.axis_size(axis)
    pairs = []
    for low in range(0 if first else 1, count, 2):
        if low + 1 < count or closed:
            high = (low + 1) % count
            pairs += [(low, high), (high, low)]
    return lax.ppermute(value, axis, pairs)


def local(adjoint_in, courant_x, courant_y, mixing, kernel_rows, tracer_weights, column_ids, counts):
    tracers, levels, lons, lats = adjoint_in.shape
    devices = lax.axis_size(("gx", "gy"))
    slots = kernel_rows.shape[1]
    fields = tracers * levels
    size = fields * lons * lats * 4

    packed = pl.pallas_call(
        pack_kernel,
        grid=(2,),
        in_specs=[
            pl.BlockSpec(memory_space=pltpu.SMEM),
            pl.BlockSpec((levels, slots // 2), lambda i: (0, i)),
            pl.BlockSpec((tracers, slots // 2), lambda i: (0, i)),
        ],
        out_specs=pl.BlockSpec((devices // 2, 24, 128), lambda i: (i, 0, 0)),
        out_shape=shape((devices, 24, 128), bf16),
        scratch_shapes=[pltpu.VMEM((512, 512), bf16)],
        compiler_params=params(60),
        name="pack",
    )(counts, kernel_rows, tracer_weights)
    got = lax.all_to_all(packed, ("gx", "gy"), split_axis=0, concat_axis=0, tiled=True)

    inv, q = pl.pallas_call(
        factor_kernel,
        out_shape=[shape((levels, lons, lats))] * 2,
        compiler_params=params(16),
        cost_estimate=cost(30 * levels * lons * lats, 3 * levels * lons * lats * 4),
        name="factor",
    )(mixing)
    bins = jnp.broadcast_to((column_ids // (2 * lats)).astype(bf16)[:, None], (slots, 128))
    code, starts = pl.pallas_call(
        rank_kernel,
        out_shape=[shape((slots, 128), bf16), shape((8 * (slots // CHUNK), 128), jnp.int32)],
        compiler_params=params(16),
        cost_estimate=cost(10**9, 2 * 10**6),
        name="rank",
    )(bins)
    lhs, places = pl.pallas_call(
        order_kernel,
        out_shape=[shape((2 * fields, slots), bf16), shape((8, slots))],
        scratch_shapes=[pltpu.VMEM((512, 512), bf16), pltpu.VMEM((80, slots), f32)],
        compiler_params=params(24),
        cost_estimate=cost(10**9, 8 * 10**6),
        name="order",
    )(got, column_ids.reshape(1, slots), code)

    vmem = pl.BlockSpec(memory_space=pltpu.VMEM)
    edge = shape((4, fields, lats), bf16)
    smem = pl.BlockSpec(memory_space=pltpu.SMEM)
    forcing_args = [starts, lhs, places, adjoint_in.reshape(fields, lons, lats)]

    def forcing(outer, *more):
        def kernel(*refs):
            forcing_kernel(outer, *refs)

        return pl.pallas_call(
            kernel,
            in_specs=[smem, vmem, vmem, pl.BlockSpec(memory_space=pl.ANY)] + [vmem] * len(more),
            out_specs=[vmem] * (3 if outer else 1),
            out_shape=[shape((fields, lons, lats))] + [edge] * (2 if outer else 0),
            input_output_aliases={} if outer else {4: 0},
            scratch_shapes=[
                pltpu.VMEM((2, fields, 8, lats), f32),
                pltpu.VMEM((fields * 9, lats), f32),
                pltpu.SemaphoreType.DMA((2,)),
            ],
            compiler_params=params(44),
            cost_estimate=cost(5 * 10**9, size),
            name="forcing",
        )(*forcing_args, *more)

    state, x_a, x_b = forcing(True)
    (state,) = forcing(False, state)

    whole_field = shape((tracers, levels, lons, lats))
    blocks = levels // LB
    note = shape((blocks, lons, 128), bf16)
    spread = jnp.asarray(edge_weights(), bf16)
    table = lat_weights()
    for step in range(STEPS):
        got_b = swap(x_b, "gx", False, True)
        got_a = swap(x_a, "gx", True, True)
        halves = pltpu.VMEM((tracers * LB * 16, 2 * lats), bf16)
        state = state.reshape(tracers, levels, lons, lats)
        partial = pl.pallas_call(
            inner_kernel,
            in_specs=[vmem] * 3,
            out_specs=[vmem] * 3,
            out_shape=[whole_field, note, note],
            scratch_shapes=[halves],
            compiler_params=params(24),
            cost_estimate=cost(5 * size, 2 * size),
            name="inner",
        )(state, courant_x, spread)
        zonal, to_a, to_b = pl.pallas_call(
            outer_kernel,
            in_specs=[vmem] * 8,
            out_specs=[vmem] * 3,
            out_shape=[whole_field, note, note],
            input_output_aliases={5: 0, 6: 1, 7: 2},
            scratch_shapes=[halves, pltpu.VMEM((tracers * LB * 33, lats), f32)],
            compiler_params=params(24),
            cost_estimate=cost(5 * size, 2 * size),
            name="outer",
        )(
            state,
            courant_x,
            spread,
            got_a.reshape(4, tracers, levels, lats),
            got_b.reshape(4, tracers, levels, lats),
            *partial,
        )
        y_b = swap(to_b, "gy", False, False)
        y_a = swap(to_a, "gy", True, False)
        inner = pl.pallas_call(
            lat_kernel,
            in_specs=[vmem] * 3,
            out_specs=vmem,
            out_shape=whole_field,
            scratch_shapes=[pltpu.VMEM((LB * tracers * lons, 2 * lats), bf16)],
            compiler_params=params(24),
            cost_estimate=cost(5 * size, 2 * size),
            name="lat",
        )(zonal, courant_y, jnp.asarray(table[:256], bf16))
        first = step == 0
        operands = [inner, courant_y, mixing, inv, q, y_a, y_b, jnp.asarray(table[256:], bf16)]
        gradient_shape = shape((tracers, lons, lats))

        def column(pieces, operands, extra, aliases):
            def kernel(*refs):
                column_kernel(pieces, first, *refs)

            rows = sum(count for _, count in pieces)
            return pl.pallas_call(
                kernel,
                in_specs=[vmem] * len(operands),
                out_specs=[vmem] * (2 + len(extra)),
                out_shape=[whole_field, gradient_shape] + extra,
                input_output_aliases=aliases,
                scratch_shapes=[pltpu.VMEM((levels * tracers * rows, 2 * lats), bf16)],
                compiler_params=params(24),
                cost_estimate=cost(5 * size, 2 * size),
                name="column",
            )(*operands)

        if first:
            state, gradient, x_a, x_b = column(((0, 8), (24, 8)), operands, [edge, edge], {})
            state, gradient = column(((8, 16),), operands + [state, gradient], [], {8: 0, 9: 1})
        else:
            state, gradient = column(((0, 32),), operands + [gradient], [], {})
    return state, gradient


def solution(mesh):
    in_specs = (
        P(None, None, "gx", "gy"),
        P(None, "gx", "gy"),
        P(None, "gx", "gy"),
        P(None, "gx", "gy"),
        P(None, ("gx", "gy")),
        P(None, ("gx", "gy")),
        P(("gx", "gy")),
        P(("gx", "gy"), None),
    )
    out_specs = (P(None, None, "gx", "gy"), P(None, "gx", "gy"))
    return jax.shard_map(local, mesh=mesh, in_specs=in_specs, out_specs=out_specs, check_vma=False)
```

```python
import jax
import jax.numpy as jnp
import numpy as np
from jax import lax
from jax.experimental import pallas as pl
from jax.experimental.pallas import tpu as pltpu
from jax.sharding import PartitionSpec as P

STEPS = 2
LB = 8
CHUNK = 1024

D1, D2, D3 = 0.75, -0.15, 1.0 / 60.0
E1, E2, E3 = 1.5, -0.15, 1.0 / 90.0
E0 = -49.0 / 18.0

f32 = jnp.float32
bf16 = jnp.bfloat16


def fill_swap(table):
    row = lax.broadcasted_iota(jnp.int32, table.shape, 0)
    col = lax.broadcasted_iota(jnp.int32, table.shape, 1)
    want = ((col >> 5) & 3) * 128 + (col >> 7) * 32 + (col & 31)
    table[...] = jnp.where(row == want, 1.0, 0.0).astype(bf16)


def is_odd(axis):
    return (lax.axis_index(axis) & 1) == 1


def split(value):
    hi = value.astype(bf16)
    return hi, (value - hi.astype(f32)).astype(bf16)


def pack_kernel(counts, rows, weights, out, swap):
    step = pl.program_id(0)
    groups = rows.shape[1] // 128

    @pl.when(step == 0)
    def _():
        fill_swap(swap)

    lane = lax.broadcasted_iota(jnp.int32, (24, 128), 1)
    block = lane >> 5
    columns = [[] for _ in range(4)]
    for g in range(groups):
        lanes = slice(g * 128, g * 128 + 128)
        first = 4 * (step * groups + g)
        limit = jnp.where(
            block < 2,
            jnp.where(block == 0, counts[0, first], counts[0, first + 1]),
            jnp.where(block == 2, counts[0, first + 2], counts[0, first + 3]),
        )
        live = (lane & 31) < limit
        for q in range(3):
            columns[q].append(jnp.where(live, rows[24 * q : 24 * q + 24, lanes].astype(f32), 0.0))
        columns[3].append(jnp.concatenate([weights[:, lanes].astype(f32), jnp.zeros((20, 128), f32)], axis=0))
    wide = jnp.concatenate([jnp.concatenate(c, axis=0).astype(bf16) for c in columns], axis=1)
    moved = jnp.dot(wide, swap[...], preferred_element_type=f32)
    for g in range(groups):
        for i in range(4):
            out[4 * g + i] = moved[24 * g : 24 * g + 24, 128 * i : 128 * i + 128].astype(bf16)


def factor_kernel(mixing, inv_out, q_out):
    levels = inv_out.shape[0]
    top = mixing[0]
    inv = 1.0 / (1.0 + top)
    q = top * inv
    inv_out[0] = inv
    q_out[0] = q

    def level(l, carry):
        below, q = carry
        above = mixing[l]
        inv = 1.0 / (1.0 + below + above - below * q)
        q = above * inv
        inv_out[l] = inv
        q_out[l] = q
        return above, q

    below, q = lax.fori_loop(1, levels - 1, level, (top, q))
    inv_out[levels - 1] = 1.0 / (1.0 + below - below * q)
    q_out[levels - 1] = jnp.zeros_like(q)


def rank_kernel(bins, code, starts):
    piece = 256
    lane = lax.broadcasted_iota(jnp.int32, (piece, 128), 1)
    lane_f = lane.astype(f32)
    upto = (lax.broadcasted_iota(jnp.int32, (piece, piece), 1) <= lax.broadcasted_iota(jnp.int32, (piece, piece), 0))
    upto = jnp.where(upto, 1.0, 0.0).astype(bf16)
    row2 = lax.broadcasted_iota(jnp.int32, (256, 256), 0)
    col2 = lax.broadcasted_iota(jnp.int32, (256, 256), 1)
    spread = jnp.where((row2 >> 7) == (col2 >> 7), 1.0, 0.0).astype(bf16)
    ones = jnp.ones((8, CHUNK), bf16)
    for h in range(bins.shape[0] // CHUNK):
        own = bins[h * CHUNK : (h + 1) * CHUNK, :].astype(f32)
        wide = lax.broadcasted_iota(jnp.int32, own.shape, 1).astype(f32)
        below = jnp.where(own < wide, 1.0, 0.0).astype(bf16)
        start = jnp.dot(ones, below, preferred_element_type=f32)
        starts[8 * h : 8 * h + 8, :] = start.astype(jnp.int32)
        running = start[0:1, :] - 1.0
        for p in range(CHUNK // piece):
            at = slice(p * piece, p * piece + piece)
            mine = own[at] == lane_f
            one_hot = jnp.where(mine, 1.0, 0.0)
            place = jnp.dot(upto, one_hot.astype(bf16), preferred_element_type=f32) + running
            running = place[piece - 1 : piece, :]
            place = jnp.where(mine, place, 0.0)
            high = jnp.floor(place * (1.0 / 128.0))
            low = place - 128.0 * high
            both = jnp.dot(
                jnp.concatenate([high.astype(bf16), low.astype(bf16)], axis=1), spread, preferred_element_type=f32
            )
            found = jnp.where(both[:, 128:] == lane_f, both[:, :128], -1.0)
            code[h * CHUNK + p * piece : h * CHUNK + (p + 1) * piece, :] = found.astype(bf16)


def order_kernel(got, ids, code, lhs, places, swap, raw):
    half = lhs.shape[0] // 2
    slots = lhs.shape[1]
    fill_swap(swap)
    batch = 8
    for first in range(0, slots // 128, batch):
        wide = jnp.concatenate(
            [
                jnp.concatenate([got[4 * (first + g) + i].astype(f32) for g in range(batch)], axis=0).astype(bf16)
                for i in range(4)
            ],
            axis=1,
        )
        moved = jnp.dot(wide, swap[...], preferred_element_type=f32)
        for g in range(batch):
            lanes = slice((first + g) * 128, (first + g) * 128 + 128)
            for q in range(4):
                count = 24 if q < 3 else 8
                raw[24 * q : 24 * q + count, lanes] = moved[24 * g : 24 * g + count, 128 * q : 128 * q + 128]
    cells = ids[...]
    raw[76:77, :] = (cells & 127).astype(f32)
    raw[77:78, :] = (cells >> 7).astype(f32)
    one, zero = jnp.ones((), bf16), jnp.zeros((), bf16)
    for h in range(slots // CHUNK):
        block = raw[:, h * CHUNK : (h + 1) * CHUNK].astype(bf16)
        part = code[h * CHUNK : (h + 1) * CHUNK, :]
        for p in range(CHUNK // 256):
            one_hot = jnp.concatenate(
                [jnp.where(part == jnp.asarray(2 * p + a, bf16), one, zero) for a in range(2)], axis=1
            )
            done = jnp.dot(block, one_hot, preferred_element_type=f32)
            lanes = slice(h * CHUNK + p * 256, h * CHUNK + (p + 1) * 256)
            places[:, lanes] = done[72:80, :]
            for t in range(4):
                hi, lo = split(done[:72] * done[72 + t : 73 + t, :])
                lhs[72 * t : 72 * t + 72, lanes] = hi
                lhs[half + 72 * t : half + 72 * t + 72, lanes] = lo


def forcing_kernel(outer, starts, lhs, places, adjoint_hbm, *rest):
    if outer:
        state, x_a, x_b, adjoint, turned, arrived = rest
        order = (0, 3)
    else:
        _, state, adjoint, turned, arrived = rest
        order = (1, 2)
    copies = [
        pltpu.make_async_copy(adjoint_hbm.at[:, pl.ds(8 * step, 8), :], adjoint.at[n], arrived.at[n])
        for n, step in enumerate(order)
    ]
    for copy in copies:
        copy.start()
    fields = state.shape[0]
    chunks = lhs.shape[1] // CHUNK
    last = CHUNK // 128 - 2
    row = lax.broadcasted_iota(jnp.int32, (128, 256), 0).astype(f32)
    window = lax.broadcasted_iota(jnp.int32, (1, 256), 1)

    def placed(base, lon, skip):
        lat = places[4:5, pl.ds(base, 256)]
        slot_lon = places[5:6, pl.ds(base, 256)]
        if skip is not None:
            slot_lon = jnp.where(window >= skip, slot_lon, -1.0)
        return jnp.concatenate(
            [
                jnp.where(jnp.where(slot_lon == (lon + a).astype(f32), lat, -1.0) == row, 1.0, 0.0).astype(bf16)
                for a in range(2)
            ],
            axis=0,
        )

    def product(bases, one_hots):
        values = [lhs[at, pl.ds(base, 256)] for at in (slice(0, fields), slice(fields, 2 * fields)) for base in bases]
        return lax.dot_general(
            jnp.concatenate(values, axis=1),
            jnp.concatenate(one_hots * 2, axis=1),
            (((1,), (1,)), ((), ())),
            preferred_element_type=f32,
        )

    def extent(h, number):
        low = starts[8 * h, number]
        high = starts[8 * h, number + 1]
        first = jnp.minimum(low >> 7, last)
        return first, jnp.maximum(((high + 127) >> 7) - first - 1, 0) >> 1

    def eight(n, _):
        step = order[0] + n * (order[1] - order[0])
        rest = jnp.int32(0)
        for pair in range(4):
            number = step * 4 + pair
            bases = []
            for h in range(chunks):
                first, visits = extent(h, number)
                rest = rest + visits
                bases.append(pl.multiple_of(h * CHUNK + first * 128, 128))
            total = product(bases, [placed(base, 2 * number, None) for base in bases])
            for a in range(2):
                turned[pl.ds(2 * pair + a, fields, stride=9), :] = total[:, 128 * a : 128 * a + 128]

        @pl.when(rest > 0)
        def _():
            def each(n, _):
                pair, h = n // chunks, n % chunks
                number = step * 4 + pair
                first, visits = extent(h, number)

                def more(j, _):
                    at = first + 2 + 2 * j
                    start = jnp.minimum(at, last)
                    base = pl.multiple_of(h * CHUNK + start * 128, 128)
                    both = product([base], [placed(base, 2 * number, (at - start) * 128)])
                    for a in range(2):
                        place = pl.ds(2 * pair + a, fields, stride=9)
                        turned[place, :] = turned[place, :] + both[:, 128 * a : 128 * a + 128]
                    return 0

                lax.fori_loop(0, visits, more, 0)
                return 0

            lax.fori_loop(0, 4 * chunks, each, 0)

        for k in range(2):

            @pl.when(n == k)
            def _(k=k):
                copies[k].wait()

        rows = pl.ds(pl.multiple_of(8 * step, 8), 8)
        for f in range(fields):
            cell = adjoint[n, f] + turned[9 * f : 9 * f + 8, :]
            state[f, rows, :] = cell
            turned[9 * f : 9 * f + 8, :] = cell

        def edge(out, order):
            near, second, third = (turned[pl.ds(j, fields, stride=9), :] for j in order)
            out[0], out[1] = split(near)
            out[2] = second.astype(bf16)
            out[3] = third.astype(bf16)

        if outer:
            odd = is_odd("gx")
            for when, sides, swapped in ((0, (0, 1, 2), odd), (1, (7, 6, 5), jnp.logical_not(odd))):
                for out, mine in ((x_a, swapped), (x_b, jnp.logical_not(swapped))):

                    @pl.when((n == when) & mine)
                    def _(out=out, sides=sides):
                        edge(out, sides)

        return 0

    lax.fori_loop(0, 2, eight, 0)


def zonal_rows(outer, state, courant, spread, halos, zonal, to_a, to_b, halves, pad):
    lane = lax.broadcasted_iota(jnp.int32, (16, 128), 1)
    group = lane >> 2
    odd_x = is_odd("gx")
    odd_y = is_odd("gy")

    def block(b, _):
        levels = pl.ds(pl.multiple_of(b * LB, LB), LB)
        if outer:
            for t in range(4):
                parts = []
                for halo in halos:
                    part = [halo[n, t, levels, :].astype(f32) for n in range(4)]
                    parts.append((part[0] + part[1], part[2], part[3]))
                for side in range(2):
                    for k in range(3):
                        value = jnp.where(odd_x, parts[side][k], parts[1 - side][k])
                        pad[pl.ds(t * LB * 33 + (24 + k if side else 7 - k), LB, stride=33), :] = value
        notes = [jnp.zeros((16, 128), f32)] * 2
        for first in range(0, LB, 4):
            for l in range(first, first + 4):
                level = b * LB + l
                if outer:
                    c = jnp.concatenate([courant[level, 0:8, :], courant[level, 24:32, :]], axis=0)
                else:
                    c = courant[level, 8:24, :]
                factors = stencil_factors(c)
                for t in range(4):
                    if outer:
                        low = state[t, level, 0:8, :]
                        high = state[t, level, 24:32, :]
                        base = 33 * (t * LB + l)
                        pad[base + 8 : base + 16, :] = low
                        pad[base + 16 : base + 24, :] = high
                        v = {0: jnp.concatenate([low, high], axis=0)}
                        for k in (1, 2, 3):
                            v[-k] = jnp.concatenate(
                                [pad[base + 8 - k : base + 16 - k, :], state[t, level, 24 - k : 32 - k, :]], axis=0
                            )
                            v[k] = jnp.concatenate(
                                [state[t, level, k : 8 + k, :], pad[base + 16 + k : base + 24 + k, :]], axis=0
                            )
                    else:
                        v = {k: state[t, level, 8 + k : 24 + k, :] for k in range(-3, 4)}
                    out = v[0] * factors[0]
                    for k in (-1, 1, -2, 2, -3, 3):
                        out = out + v[k] * factors[k]
                    if outer:
                        zonal[t, level, 0:8, :] = out[:8]
                        zonal[t, level, 24:32, :] = out[8:]
                    else:
                        zonal[t, level, 8:24, :] = out
                    at = slice(16 * (4 * l + t), 16 * (4 * l + t) + 16)
                    halves[at, 0:128], halves[at, 128:256] = split(out)
            at = slice(64 * first, 64 * first + 256)
            edges = jnp.dot(halves[at, :], spread[...], preferred_element_type=f32)
            for l in range(4):
                for t in range(4):
                    mine = group == t * LB + first + l
                    rows = slice(16 * (4 * l + t), 16 * (4 * l + t) + 16)
                    notes = [jnp.where(mine, edges[rows, 128 * n : 128 * n + 128], notes[n]) for n in range(2)]
        for out, note in (
            (to_a, jnp.where(odd_y, notes[0], notes[1]).astype(bf16)),
            (to_b, jnp.where(odd_y, notes[1], notes[0]).astype(bf16)),
        ):
            if outer:
                out[b, 0:8] = note[:8]
                out[b, 24:32] = note[8:]
            else:
                out[b, 8:24] = note
        return 0

    lax.fori_loop(0, courant.shape[0] // LB, block, 0)


def inner_kernel(state, courant, spread, zonal, to_a, to_b, halves):
    zonal_rows(False, state, courant, spread, None, zonal, to_a, to_b, halves, None)


def outer_kernel(state, courant, spread, from_a, from_b, _z, _a, _b, zonal, to_a, to_b, halves, pad):
    zonal_rows(True, state, courant, spread, (from_a, from_b), zonal, to_a, to_b, halves, pad)


def stencil_factors(c):
    c2 = 0.5 * c * c
    factors = {0: 1.0 + E0 * c2}
    for k, d, e in ((1, D1, E1), (2, D2, E2), (3, D3, E3)):
        slope, curve = d * c, e * c2
        factors[k] = curve + slope
        factors[-k] = curve - slope
    return factors


def lat_kernel(zonal, courant, weights, result, halves):
    tracers, levels, lons, lats = zonal.shape
    rows = tracers * lons

    def block(b, _):
        for l in range(LB):
            level = b * LB + l
            at = slice(l * rows, (l + 1) * rows)
            halves[at, 0:128], halves[at, 128:256] = split(zonal[:, level].reshape(rows, lats))
        for l in range(LB):
            level = b * LB + l
            at = slice(l * rows, (l + 1) * rows)
            both = jnp.dot(halves[at, :], weights[...], preferred_element_type=f32).reshape(tracers, lons, 256)
            c = courant[level]
            result[:, level] = (
                zonal[:, level] + (c * (1.0 / 60.0)) * both[:, :, :128] + (c * c * (1.0 / 360.0)) * both[:, :, 128:]
            )
        return 0

    lax.fori_loop(0, levels // LB, block, 0)


def column_kernel(pieces, first, inner, courant, mixing, inv, q, from_a, from_b, weights, *rest):
    lhs = rest[-1]
    x_a = x_b = before = None
    if not first:
        before, state, gradient = rest[:-1]
    elif len(pieces) == 2:
        state, gradient, x_a, x_b, turned = rest[:-1]
    else:
        _, _, state, gradient = rest[:-1]
    levels = inv.shape[0]
    lons = sum(count for _, count in pieces)
    rows = 4 * lons

    def get(ref, *index):
        parts = [ref[(*index, slice(start, start + count), slice(None))] for start, count in pieces]
        return parts[0] if len(parts) == 1 else jnp.concatenate(parts, axis=-2)

    def put(ref, value, *index):
        done = 0
        for start, count in pieces:
            ref[(*index, slice(start, start + count), slice(None))] = value[..., done : done + count, :]
            done += count

    lane = lax.broadcasted_iota(jnp.int32, (rows, 128), 1)
    row = lax.broadcasted_iota(jnp.int32, (rows, 128), 0)
    owner = ((lane >> 2) - (row // lons) * LB).astype(f32).astype(bf16)
    zero = jnp.zeros((), bf16)
    odd_y = is_odd("gy")

    every = slice(None)
    carry = None
    for b in range(levels // LB):
        a, z = get(from_a, b).astype(f32), get(from_b, b).astype(f32)
        notes = [
            jnp.concatenate([note] * 4, axis=0).astype(bf16) for note in (jnp.where(odd_y, a, z), jnp.where(odd_y, z, a))
        ]
        for l in range(LB):
            at = slice((b * LB + l) * rows, (b * LB + l + 1) * rows)
            mine = owner == jnp.asarray(l, bf16)
            lhs[at, 0:128] = jnp.where(mine, notes[0], zero)
            lhs[at, 128:256] = jnp.where(mine, notes[1], zero)
        both = jnp.dot(lhs[b * LB * rows : (b + 1) * LB * rows, :], weights[...], preferred_element_type=f32)
        for l in range(LB):
            level = b * LB + l
            c = get(courant, level)
            part = both[l * rows : l * rows + rows].reshape(4, lons, 256)
            y = get(inner, every, level)
            y = y + (c * (1.0 / 60.0)) * part[:, :, :128] + (c * c * (1.0 / 360.0)) * part[:, :, 128:]
            if level > 0:
                y = y + get(mixing, level - 1) * carry
            carry = y * get(inv, level)
            put(state, carry, every, level)

    def keep(carry, level):
        if x_a is not None:
            for t in range(4):
                for side in range(2):
                    place = pl.ds(9 * (levels * t + level), 8)
                    turned[side, place, :] = carry[t, 8 * side : 8 * side + 8]

    def back(j, carry):
        level = levels - 2 - j
        carry = get(state, every, level) + get(q, level) * carry
        put(state, carry, every, level)
        keep(carry, level)
        return carry

    keep(carry, levels - 1)

    carry = lax.fori_loop(0, levels - 1, back, carry, unroll=8)
    put(gradient, carry if first else get(before, every) + carry, every)
    if x_a is not None:

        def edge(out, order):
            for t in range(4):
                rows = slice(levels * t, levels * t + levels)
                near, second, third = (
                    turned[order[0] // 16, pl.ds(9 * levels * t + j % 8, levels, stride=9), :] for j in order
                )
                out[0, rows], out[1, rows] = split(near)
                out[2, rows] = second.astype(bf16)
                out[3, rows] = third.astype(bf16)

        low, high = (0, 1, 2), (31, 30, 29)

        @pl.when(is_odd("gx"))
        def _():
            edge(x_a, low)
            edge(x_b, high)

        @pl.when(jnp.logical_not(is_odd("gx")))
        def _():
            edge(x_a, high)
            edge(x_b, low)


def edge_weights():
    table = np.zeros((256, 256), np.float32)
    for lane in range(128):
        part = lane % 4
        table[(128, part)[part < 3], lane] = 1
        table[(255, 125 + part)[part < 3], 128 + lane] = 1
    return table


def lat_weights():
    first = {1: 45, 2: -9, 3: 1}
    second = {0: -490, 1: 270, 2: -27, 3: 2}
    table = np.zeros((512, 256), np.float32)

    def fill(row, place):
        for out in range(128):
            k = place - out
            if abs(k) <= 3:
                table[row, out] = first.get(abs(k), 0) * (1 if k > 0 else -1)
                table[row, 128 + out] = second[abs(k)]

    for lane in range(128):
        fill(lane, lane)
        fill(128 + lane, lane)
        fill(256 + lane, (-3, -2, -1, -1)[lane % 4])
        fill(384 + lane, (128, 129, 130, 128)[lane % 4])
    return table


def cost(flops, size):
    return pl.CostEstimate(flops=flops, bytes_accessed=size, transcendentals=0)


def params(mib):
    return pltpu.CompilerParams(vmem_limit_bytes=mib * 2**20)


def shape(dims, kind=f32):
    return jax.ShapeDtypeStruct(dims, kind)


def swap(value, axis, first, closed):
    count = lax.axis_size(axis)
    pairs = []
    for low in range(0 if first else 1, count, 2):
        if low + 1 < count or closed:
            high = (low + 1) % count
            pairs += [(low, high), (high, low)]
    return lax.ppermute(value, axis, pairs)


def local(adjoint_in, courant_x, courant_y, mixing, kernel_rows, tracer_weights, column_ids, counts):
    tracers, levels, lons, lats = adjoint_in.shape
    devices = lax.axis_size(("gx", "gy"))
    slots = kernel_rows.shape[1]
    fields = tracers * levels
    size = fields * lons * lats * 4

    packed = pl.pallas_call(
        pack_kernel,
        grid=(2,),
        in_specs=[
            pl.BlockSpec(memory_space=pltpu.SMEM),
            pl.BlockSpec((levels, slots // 2), lambda i: (0, i)),
            pl.BlockSpec((tracers, slots // 2), lambda i: (0, i)),
        ],
        out_specs=pl.BlockSpec((devices // 2, 24, 128), lambda i: (i, 0, 0)),
        out_shape=shape((devices, 24, 128), bf16),
        scratch_shapes=[pltpu.VMEM((512, 512), bf16)],
        compiler_params=params(60),
        name="pack",
    )(counts, kernel_rows, tracer_weights)
    got = lax.all_to_all(packed, ("gx", "gy"), split_axis=0, concat_axis=0, tiled=True)

    inv, q = pl.pallas_call(
        factor_kernel,
        out_shape=[shape((levels, lons, lats))] * 2,
        compiler_params=params(16),
        cost_estimate=cost(30 * levels * lons * lats, 3 * levels * lons * lats * 4),
        name="factor",
    )(mixing)
    bins = jnp.broadcast_to((column_ids // (2 * lats)).astype(bf16)[:, None], (slots, 128))
    code, starts = pl.pallas_call(
        rank_kernel,
        out_shape=[shape((slots, 128), bf16), shape((8 * (slots // CHUNK), 128), jnp.int32)],
        compiler_params=params(16),
        cost_estimate=cost(10**9, 2 * 10**6),
        name="rank",
    )(bins)
    lhs, places = pl.pallas_call(
        order_kernel,
        out_shape=[shape((2 * fields, slots), bf16), shape((8, slots))],
        scratch_shapes=[pltpu.VMEM((512, 512), bf16), pltpu.VMEM((80, slots), f32)],
        compiler_params=params(24),
        cost_estimate=cost(10**9, 8 * 10**6),
        name="order",
    )(got, column_ids.reshape(1, slots), code)

    vmem = pl.BlockSpec(memory_space=pltpu.VMEM)
    edge = shape((4, fields, lats), bf16)
    smem = pl.BlockSpec(memory_space=pltpu.SMEM)
    forcing_args = [starts, lhs, places, adjoint_in.reshape(fields, lons, lats)]

    def forcing(outer, *more):
        def kernel(*refs):
            forcing_kernel(outer, *refs)

        return pl.pallas_call(
            kernel,
            in_specs=[smem, vmem, vmem, pl.BlockSpec(memory_space=pl.ANY)] + [vmem] * len(more),
            out_specs=[vmem] * (3 if outer else 1),
            out_shape=[shape((fields, lons, lats))] + [edge] * (2 if outer else 0),
            input_output_aliases={} if outer else {4: 0},
            scratch_shapes=[
                pltpu.VMEM((2, fields, 8, lats), f32),
                pltpu.VMEM((fields * 9, lats), f32),
                pltpu.SemaphoreType.DMA((2,)),
            ],
            compiler_params=params(44),
            cost_estimate=cost(5 * 10**9, size),
            name="forcing",
        )(*forcing_args, *more)

    state, x_a, x_b = forcing(True)
    (state,) = forcing(False, state)

    whole_field = shape((tracers, levels, lons, lats))
    blocks = levels // LB
    note = shape((blocks, lons, 128), bf16)
    spread = jnp.asarray(edge_weights(), bf16)
    table = lat_weights()
    for step in range(STEPS):
        got_b = swap(x_b, "gx", False, True)
        got_a = swap(x_a, "gx", True, True)
        halves = pltpu.VMEM((tracers * LB * 16, 2 * lats), bf16)
        state = state.reshape(tracers, levels, lons, lats)
        partial = pl.pallas_call(
            inner_kernel,
            in_specs=[vmem] * 3,
            out_specs=[vmem] * 3,
            out_shape=[whole_field, note, note],
            scratch_shapes=[halves],
            compiler_params=params(24),
            cost_estimate=cost(5 * size, 2 * size),
            name="inner",
        )(state, courant_x, spread)
        zonal, to_a, to_b = pl.pallas_call(
            outer_kernel,
            in_specs=[vmem] * 8,
            out_specs=[vmem] * 3,
            out_shape=[whole_field, note, note],
            input_output_aliases={5: 0, 6: 1, 7: 2},
            scratch_shapes=[halves, pltpu.VMEM((tracers * LB * 33, lats), f32)],
            compiler_params=params(24),
            cost_estimate=cost(5 * size, 2 * size),
            name="outer",
        )(
            state,
            courant_x,
            spread,
            got_a.reshape(4, tracers, levels, lats),
            got_b.reshape(4, tracers, levels, lats),
            *partial,
        )
        y_b = swap(to_b, "gy", False, False)
        y_a = swap(to_a, "gy", True, False)
        inner = pl.pallas_call(
            lat_kernel,
            in_specs=[vmem] * 3,
            out_specs=vmem,
            out_shape=whole_field,
            scratch_shapes=[pltpu.VMEM((LB * tracers * lons, 2 * lats), bf16)],
            compiler_params=params(24),
            cost_estimate=cost(5 * size, 2 * size),
            name="lat",
        )(zonal, courant_y, jnp.asarray(table[:256], bf16))
        first = step == 0
        operands = [inner, courant_y, mixing, inv, q, y_a, y_b, jnp.asarray(table[256:], bf16)]
        gradient_shape = shape((tracers, lons, lats))

        def column(pieces, operands, extra, aliases):
            def kernel(*refs):
                column_kernel(pieces, first, *refs)

            rows = sum(count for _, count in pieces)
            return pl.pallas_call(
                kernel,
                in_specs=[vmem] * len(operands),
                out_specs=[vmem] * (2 + len(extra)),
                out_shape=[whole_field, gradient_shape] + extra,
                input_output_aliases=aliases,
                scratch_shapes=([pltpu.VMEM((2, fields * 9, lats), f32)] if extra else [])
                + [pltpu.VMEM((levels * tracers * rows, 2 * lats), bf16)],
                compiler_params=params(24),
                cost_estimate=cost(5 * size, 2 * size),
                name="column",
            )(*operands)

        if first:
            state, gradient, x_a, x_b = column(((0, 8), (24, 8)), operands, [edge, edge], {})
            state, gradient = column(((8, 16),), operands + [state, gradient], [], {8: 0, 9: 1})
        else:
            state, gradient = column(((0, 32),), operands + [gradient], [], {})
    return state, gradient


def solution(mesh):
    in_specs = (
        P(None, None, "gx", "gy"),
        P(None, "gx", "gy"),
        P(None, "gx", "gy"),
        P(None, "gx", "gy"),
        P(None, ("gx", "gy")),
        P(None, ("gx", "gy")),
        P(("gx", "gy")),
        P(("gx", "gy"), None),
    )
    out_specs = (P(None, None, "gx", "gy"), P(None, "gx", "gy"))
    return jax.shard_map(local, mesh=mesh, in_specs=in_specs, out_specs=out_specs, check_vma=False)
```
